256 devices in a mesh: ctx: 32 (over z, x), head: 8 (over y, core).
Axes of the slice: x: 4, y: 4, z: 8, core: 2. Of those that a mesh axis runs over, the one named last changes fastest.
Arguments:
- queries: bfloat16 [3, 64, 12288], P(None, None, 'head'), may hold values from -96 to 96
- key_latent: bfloat16 [8, 65536, 256], P('head', 'ctx'), may hold values from -6 to 6
- value_latent: bfloat16 [8, 65536, 256], P('head', 'ctx'), may hold values from -6 to 6
- key_up: bfloat16 [8, 256, 128], P('head'), may hold values from -0.375 to 0.375
- value_up: bfloat16 [8, 256, 128], P('head'), may hold values from -0.375 to 0.375
- out_weight: bfloat16 [12288, 12288], P('head', 'ctx'), may hold values from -0.0546875 to 0.0546875
- prior_scores: float32 [8, 65536], P('head', 'ctx'), may hold values from 0 to 2
- lengths: int32 [3], replicated, may hold values from 49152 to 65536, as said below
- positions: int32 [3, 64], replicated, may hold values from 49152 to 65599, as said below
Outputs:
- attended: bfloat16 [3, 64, 12288], P(None, 'head', 'ctx')
- eviction: float32 [8, 65536], P('head', 'ctx')
The draws below stay inside these ranges and needn't reach their ends.
Inputs may be any that keep to these rules, and one draw needn't show every extreme that they name: `lengths`: later steps have more valid tokens; the last step has all 65536. Within a step the positions start at that step's valid length and never fall, rising by at most one from a row to the next; in the last step they rise by exactly one each row.
All inputs are finite; a program needn't handle non-finite values.
Results may differ from the reference program's by a relative error of at most 0.028.
Values may be sent and summed in bfloat16 or wider, within the bound.
A program may use at most 128 MiB of HBM per device.

```python
import jax
import jax.numpy as jnp
from jax import lax

D = 12288
G = 8
HPG = 12
HD = 128
R = 256
STEPS = 3
Q = 64
CTX = 65536


def valid_counts(key):
    extra = jax.random.randint(key, (STEPS,), 0, CTX // 8)
    order = jnp.arange(STEPS, dtype=jnp.int32)
    extra = jnp.where(order < STEPS - 1, extra, 0)
    return (CTX - (STEPS - 1 - order) * (CTX // 8) + extra).astype(jnp.int32)


def draw_lengths(key, part):
    counts = valid_counts(key)
    return counts


def draw_positions(key, part):
    counts = valid_counts(key)
    key = jax.random.fold_in(key, 5)
    rises = jax.random.randint(key, (STEPS, Q), 0, 2)
    row_step = jnp.arange(STEPS, dtype=jnp.int32)[:, None]
    rises = jnp.where(row_step == STEPS - 1, 1, rises)
    column = jnp.arange(Q, dtype=jnp.int32)[None, :]
    rises = jnp.where(column == 0, 0, rises)
    return (counts[:, None] + jnp.cumsum(rises, axis=1)).astype(jnp.int32)


def draw_queries(key, part):
    key = jax.random.fold_in(key, 3)
    shape = (STEPS, Q, G * HPG * HD)
    values = jax.random.normal(key, shape, jnp.float32) * 3.0
    return jnp.clip(values, -96.0, 96.0).astype(jnp.bfloat16)


def levels(stream_key, extent, cuts, smallest, largest):
    factor_of = 1.0
    for position, parts in cuts:
        draws = jax.random.uniform(jax.random.fold_in(jax.random.fold_in(stream_key, 6), position), (parts,), jnp.float32, smallest / len(cuts), largest / len(cuts))
        factor_of = factor_of * jnp.repeat(jnp.exp(draws), extent[position] // parts).reshape((-1,) + (1,) * (len(extent) - 1 - position))
    return factor_of


def bell_draw(stream_key, shape, spread, reach, shards=(), kind=jnp.bfloat16):
    drawn = jax.random.normal(stream_key, shape, jnp.float32) * spread
    if len(shards) > 0:
        drawn = levels(stream_key, shape, shards, -0.22, 0.18) * drawn
    return jnp.clip(drawn, min=-reach, max=reach).astype(kind)


def setup_inputs(seed: int = 0) -> dict:
    key_of = jax.random.split(jax.random.key(seed), 10)
    queries = draw_queries(jax.random.fold_in(key_of[9], 71), 0)
    key_latent = bell_draw(key_of[1], (G, CTX, R), 1.0, 6.0, ((0, 8), (1, 32)))
    value_latent = bell_draw(key_of[2], (G, CTX, R), 1.0, 6.0, ((0, 8), (1, 32)))
    key_up = bell_draw(key_of[3], (G, R, HD), R ** -0.5, 0.375, ((0, 8),))
    value_up = bell_draw(key_of[4], (G, R, HD), R ** -0.5, 0.375, ((0, 8),))
    out_weight = bell_draw(key_of[5], (G * HPG * HD, D), (G * HPG * HD) ** -0.5, 0.0546875, ((0, 8), (1, 32)))
    prior_scores = jnp.clip(2.0 * jax.random.uniform(key_of[6], (G, CTX), jnp.float32) ** levels(key_of[6], (G, CTX), ((0, 8), (1, 32)), -0.2, 0.2), 0.0, 2.0)
    lengths = draw_lengths(jax.random.fold_in(key_of[9], 71), 0)
    positions = draw_positions(jax.random.fold_in(key_of[9], 71), 0)
    return dict(queries=queries, key_latent=key_latent, value_latent=value_latent, key_up=key_up, value_up=value_up, out_weight=out_weight, prior_scores=prior_scores, lengths=lengths, positions=positions)


ROPE_BASE = 1000000.0
NEGATIVE = -1e30


def rotate(vectors, where_at):
    half = vectors.shape[-1] // 2
    freq = ROPE_BASE ** (-(jnp.arange(half, dtype=jnp.float32) * 2.0 / vectors.shape[-1]))
    angle = where_at.astype(jnp.float32)[:, None] * freq[None, :]
    cosine = jnp.cos(angle)
    sine = jnp.sin(angle)
    first = vectors[..., :half]
    second = vectors[..., half:]
    return jnp.concatenate([first * cosine - second * sine, second * cosine + first * sine], axis=-1)


def reference(queries, key_latent, value_latent, key_up, value_up, out_weight, prior_scores, lengths, positions):
    key_pos = jnp.arange(CTX, dtype=jnp.int32)
    keys = jnp.einsum("gkr,grd->gkd", key_latent.astype(jnp.float32), key_up.astype(jnp.float32))
    keys = rotate(keys, key_pos).astype(jnp.bfloat16)
    values = jnp.einsum("gkr,grd->gkd", value_latent.astype(jnp.float32), value_up.astype(jnp.float32)).astype(jnp.bfloat16)
    tally = prior_scores
    results = []
    for step in range(STEPS):
        query_f = queries[step].astype(jnp.float32).reshape(Q, G * HPG, HD).transpose(1, 0, 2)
        query_b = (rotate(query_f, positions[step]) * (HD ** -0.5)).astype(jnp.bfloat16)
        live = key_pos < lengths[step]

        def one_head(index):
            group = index // HPG
            key_g = lax.dynamic_index_in_dim(keys, group, 0, keepdims=False)
            value_g = lax.dynamic_index_in_dim(values, group, 0, keepdims=False)
            query_h = lax.dynamic_index_in_dim(query_b, index, 0, keepdims=False)
            scores = jnp.dot(query_h, key_g.T, preferred_element_type=jnp.float32)
            scores = jnp.where(live[None, :], scores, NEGATIVE)
            top = jnp.max(scores, axis=1, keepdims=True)
            expo = jnp.where(live[None, :], jnp.exp(scores - top), 0.0)
            total = jnp.sum(expo, axis=1, keepdims=True)
            weights = expo.astype(jnp.bfloat16)
            heads_out = (jnp.dot(weights, value_g, preferred_element_type=jnp.float32) / total).astype(jnp.bfloat16)
            column = jnp.sum(weights.astype(jnp.float32) / total, axis=0)
            return heads_out, column

        heads_out, column = lax.map(one_head, jnp.arange(G * HPG, dtype=jnp.int32))
        tally = tally + jnp.sum(column.reshape(G, HPG, CTX), axis=1)
        flat = heads_out.transpose(1, 0, 2).reshape(Q, G * HPG * HD)
        results.append(jnp.dot(flat, out_weight, preferred_element_type=jnp.float32).astype(jnp.bfloat16))
    return jnp.stack(results), tally
```

```python
import functools

import jax
import jax.numpy as jnp
import numpy as np
from jax import lax
from jax.experimental import pallas as pl
from jax.experimental.pallas import tpu as pltpu
from jax.sharding import PartitionSpec as P

ROPE_BASE = 1000000.0
NEGATIVE = -1e30
BF16 = jnp.bfloat16
F32 = jnp.float32
MESH = pl.DeviceIdType.MESH

NX, NZ, NHEAD = 4, 8, 8
STEPS, ROWS = 3, 64
HEADS, DIM, RANK = 12, 128, 256
TOKENS = 2048
WIDTH = 384
LIVE = STEPS * (ROWS // NZ)
BLOCK = LIVE + 8
PAD = NZ * BLOCK
HROWS = STEPS * ROWS
PAIR = 2
GROUP = NX
GROUPS = HEADS // GROUP
UNITS = HEADS // PAIR
LANES = 128


def rotary_tables():
    half = DIM // 2
    freq = (ROPE_BASE ** (-(np.arange(half) * 2.0 / DIM))).astype(np.float32).astype(np.float64)
    starts = np.arange(NX * NZ * TOKENS // LANES, dtype=np.float64) * LANES
    coarse = freq[:, None] * starts[None, :]
    coarse = coarse.reshape(half, -1, LANES).transpose(1, 0, 2)
    fine = freq[:, None] * np.arange(LANES, dtype=np.float64)[None, :]
    pair = lambda a, axis: np.stack([np.cos(a), np.sin(a)], axis=axis).astype(np.float32)
    row = np.concatenate([freq, freq]).astype(np.float32)[None, :]
    return pair(coarse, 1), pair(fine, 0), np.broadcast_to(row, (8, DIM)).copy()


def three(x):
    hi = x.astype(BF16).astype(F32)
    rest = x - hi
    mid = rest.astype(BF16).astype(F32)
    return hi, mid, rest - mid


def two(x):
    hi = x.astype(BF16).astype(F32)
    return hi, x - hi


def stack_rows(rows):
    sub = lax.broadcasted_iota(jnp.int32, (8, LANES), 0)
    out = jnp.zeros((8, LANES), F32)
    for index, row in enumerate(rows):
        out = jnp.where(sub == index, row, out)
    return out


def top_of(stats):
    return stats[0:1] + stats[1:2] + stats[2:3]


def total_of(stats):
    return stats[3:4] + stats[4:5]


def join(stats):
    tops = [top_of(s) for s in stats]
    peak = functools.reduce(jnp.maximum, tops)
    factors = [jnp.exp(t - peak) for t in tops]
    total = functools.reduce(jnp.add, [f * total_of(s) for f, s in zip(factors, stats)])
    return peak, total, factors


def kernel(
    q_hbm, kl_hbm, vl_hbm, ku_ref, vu_ref, w_hbm, prior_ref, len_ref, pos_ref, coarse_ref, fine_ref, freq_ref,
    out_ref, ev_ref,
    q_v, kl_v, vl_v, w_v, qa, keys, values, pos_v, score_a, score_b, weights, stat_v,
    xw, xr, zw, zr, ft, ax, acc, hw, hr,
    load_sem, xs_sem, xr_sem, zs_sem, zr_sem, as_sem, ar_sem, bs_sem, br_sem, hs_sem, hr_sem,
):
    ctx = lax.axis_index("ctx")
    head = lax.axis_index("head")
    z = ctx // NX
    x = lax.rem(ctx, NX)

    loads = [
        pltpu.make_async_copy(src, dst, load_sem.at[i])
        for i, (src, dst) in enumerate([(kl_hbm.at[0], kl_v), (q_hbm, q_v), (vl_hbm.at[0], vl_v), (w_hbm, w_v)])
    ]
    for load in loads:
        load.start()

    def at_x(d):
        return {"ctx": z * NX + lax.rem(x + d, NX), "head": head}

    def at_z(d):
        return {"ctx": lax.rem(z + d, NZ) * NX + x, "head": head}

    def at_head(d):
        return {"ctx": ctx, "head": lax.rem(head + d, NHEAD)}

    peers = [at_x(d) for d in range(1, NX)] + [at_z(d) for d in range(1, NZ)] + [at_head(d) for d in range(1, NHEAD)]
    barrier = pltpu.get_barrier_semaphore()
    for peer in peers:
        pl.semaphore_signal(barrier, inc=1, device_id=peer, device_id_type=MESH)

    def send(src, dst, s_sem, r_sem, peer):
        copy = pltpu.make_async_remote_copy(
            src_ref=src, dst_ref=dst, send_sem=s_sem, recv_sem=r_sem, device_id=peer, device_id_type=MESH
        )
        copy.start()
        return copy

    pos_v[...] = jnp.zeros_like(pos_v)
    pos_v[0:STEPS, 0:ROWS] = pos_ref[...].astype(F32)
    pos_t = jnp.transpose(pos_v[...])
    where_at = jnp.concatenate(
        [pos_t[8 * p : 8 * p + 8, s : s + 1] for p in range(NZ) for s in range(STEPS)], axis=0
    )
    angle = where_at * freq_ref[0:1, :]
    lane = lax.broadcasted_iota(jnp.int32, (HROWS, DIM), 1)
    cos_q = jnp.cos(angle)
    sin_q = jnp.where(lane < DIM // 2, -jnp.sin(angle), jnp.sin(angle))
    row_step = jnp.concatenate(
        [jnp.full((8, DIM), s, jnp.int32) for p in range(NZ) for s in range(STEPS)], axis=0
    )
    marks = jnp.where(lane == row_step, 1.0, 0.0).astype(BF16)

    loads[0].wait()
    key_up = jnp.transpose(ku_ref[0].astype(F32)).astype(BF16)
    coarse = coarse_ref[lax.div(ctx, 8)]
    shift = lax.rem(LANES - lax.rem(ctx, 8) * (TOKENS // LANES), LANES)
    cos_c = pltpu.roll(coarse[0], shift, 1)
    sin_c = pltpu.roll(coarse[1], shift, 1)
    cos_f = fine_ref[0]
    sin_f = fine_ref[1]
    half = DIM // 2
    chunk = 512
    for start in range(0, TOKENS, chunk):
        raw = lax.dot_general(
            key_up, kl_v[start : start + chunk, :], (((1,), (1,)), ((), ())), preferred_element_type=F32
        )
        for off in range(0, chunk, LANES):
            a = (start + off) // LANES
            ca, sa = cos_c[:, a : a + 1], sin_c[:, a : a + 1]
            cosine = ca * cos_f - sa * sin_f
            sine = sa * cos_f + ca * sin_f
            first, second = raw[:half, off : off + LANES], raw[half:, off : off + LANES]
            keys[0:half, start + off : start + off + LANES] = (first * cosine - second * sine).astype(BF16)
            keys[half:DIM, start + off : start + off + LANES] = (second * cosine + first * sine).astype(BF16)
    token = ctx * TOKENS + lax.broadcasted_iota(jnp.int32, (16, TOKENS), 1)
    step_row = lax.broadcasted_iota(jnp.int32, (16, TOKENS), 0)
    limit = jnp.where(step_row == 0, len_ref[0], jnp.where(step_row == 1, len_ref[1], len_ref[2]))
    dead = (step_row < STEPS) & (token >= limit)
    keys[DIM : DIM + 16, :] = jnp.where(dead, NEGATIVE, 0.0).astype(BF16)
    keys[DIM + 16 : 2 * DIM, :] = jnp.zeros((DIM - 16, TOKENS), BF16)

    loads[1].wait()
    for h in range(HEADS):
        block = [q_v[s, :, h * DIM : (h + 1) * DIM].astype(F32) for s in range(STEPS)]
        rows = jnp.concatenate([block[s][8 * p : 8 * p + 8] for p in range(NZ) for s in range(STEPS)], axis=0)
        turned = (rows * cos_q + pltpu.roll(rows, half, 1) * sin_q) * (DIM**-0.5)
        qa[h * HROWS : (h + 1) * HROWS, 0:DIM] = turned.astype(BF16)
        qa[h * HROWS : (h + 1) * HROWS, DIM : 2 * DIM] = marks

    loads[2].wait()
    values[...] = jnp.dot(vl_v[...], vu_ref[0], preferred_element_type=F32).astype(BF16)

    span = PAIR * HROWS

    def scores(u, dst):
        dst[...] = jnp.dot(qa[u * span : (u + 1) * span, :], keys[...], preferred_element_type=F32)

    stat_lane = lax.broadcasted_iota(jnp.int32, (HROWS, LANES), 1)
    filler = jnp.where(lax.broadcasted_iota(jnp.int32, (8, LANES), 1) == 3, 1.0, 0.0)

    def soft(u, src):
        s = src[...]
        top = jnp.max(s, axis=1, keepdims=True)
        expo = jnp.exp(s - top)
        total = jnp.sum(expo, axis=1, keepdims=True)
        w = expo.astype(BF16)
        weights[u * span : (u + 1) * span, :] = w
        sums = jnp.dot(w, values[...], preferred_element_type=F32)
        for i in range(PAIR):
            h = u * PAIR + i
            rows = slice(i * HROWS, (i + 1) * HROWS)
            columns = jnp.zeros((HROWS, LANES), F32)
            for k, part in enumerate((*three(top[rows]), *two(total[rows]))):
                columns = jnp.where(stat_lane == k, part, columns)
            spread = []
            for p in range(NZ):
                spread += [columns[LIVE * p : LIVE * (p + 1)], filler]
            stats = jnp.transpose(jnp.concatenate(spread, axis=0))[0:8]
            stat_v[h] = stats
            for p in range(NZ):
                half_stats = stats[:, LANES * (p // 4) : LANES * (p // 4 + 1)]
                piece = jnp.concatenate([sums[rows][LIVE * p : LIVE * (p + 1)], half_stats], axis=0)
                xw[h, BLOCK * p : BLOCK * (p + 1), :] = piece.astype(BF16)

    sent = []

    def send_x(g):
        for d in range(1, NX):
            there = g * GROUP + lax.rem(x + d, NX)
            sent.append(send(xw.at[there], xr.at[g, d - 1], xs_sem.at[g, d - 1], xr_sem.at[g, d - 1], at_x(d)))

    def wait_for(dst, sem):
        pltpu.make_async_copy(dst, dst, sem).wait()

    def merge_x(g):
        for d in range(1, NX):
            wait_for(xr.at[g, d - 1], xr_sem.at[g, d - 1])
        mine = g * GROUP + x

        def piece(c, p):
            ref = xw.at[mine] if c == 0 else xr.at[g, c - 1]
            return ref[BLOCK * p : BLOCK * (p + 1), :].astype(F32)

        for q in range(NZ // 4):
            first = [piece(c, 4 * q) for c in range(NX)]
            peak, total, factors = join([f[LIVE:] for f in first])
            by_row = jnp.transpose(stack_rows(factors))
            stats = stack_rows((*three(peak), *two(total)))
            for b in range(4):
                p = 4 * q + b
                merged = functools.reduce(
                    jnp.add,
                    [
                        (first[c] if b == 0 else piece(c, p))[:LIVE] * by_row[BLOCK * b : BLOCK * b + LIVE, c : c + 1]
                        for c in range(NX)
                    ],
                )
                zw[g, BLOCK * p : BLOCK * (p + 1), :] = jnp.concatenate([merged, stats], axis=0).astype(BF16)

    def send_z(g):
        for d in range(1, NZ):
            there = lax.rem(z + d, NZ)
            src = zw.at[g, pl.ds(pl.multiple_of(there * BLOCK, BLOCK), BLOCK)]
            sent.append(send(src, zr.at[g, d - 1], zs_sem.at[g, d - 1], zr_sem.at[g, d - 1], at_z(d)))

    def mine_z():
        return pl.ds(pl.multiple_of(z * BLOCK, BLOCK), BLOCK)

    def merge_z(g):
        for d in range(1, NZ):
            wait_for(zr.at[g, d - 1], zr_sem.at[g, d - 1])
        pieces = [zw[g, mine_z(), :].astype(F32)] + [zr[g, i].astype(F32) for i in range(NZ - 1)]
        peak, total, factors = join([p[LIVE:] for p in pieces])
        scale = 1.0 / total
        ft[:, 0:8] = jnp.transpose(stack_rows([f * scale for f in factors]))
        by_row = ft[pl.ds(pl.multiple_of(lax.rem(z, 4) * BLOCK, BLOCK), LIVE), 0:8]
        merged = functools.reduce(jnp.add, [p[:LIVE] * by_row[:, c : c + 1] for c, p in enumerate(pieces)])
        stats = stack_rows((*three(peak), *two(total)))
        ax[g * GROUP + x, mine_z(), :] = jnp.concatenate([merged, stats], axis=0).astype(BF16)

    def share_z(g):
        here = ax.at[g * GROUP + x, mine_z()]
        for d in range(1, NZ):
            sent.append(send(here, here, as_sem.at[g, d - 1], ar_sem.at[g, d - 1], at_z(d)))

    def share_x(g):
        for d in range(1, NZ):
            here = ax.at[g * GROUP + x, mine_z()]
            wait_for(here, ar_sem.at[g, d - 1])
        here = ax.at[g * GROUP + x]
        for d in range(1, NX):
            sent.append(send(here, here, bs_sem.at[g, d - 1], br_sem.at[g, d - 1], at_x(d)))

    def gathered(g):
        for d in range(1, NX):
            here = ax.at[g * GROUP + x]
            wait_for(here, br_sem.at[g, d - 1])

    def project(g):
        rows = jnp.concatenate([ax[g * GROUP + i] for i in range(GROUP)], axis=1)
        part = jnp.dot(rows, w_v[g * GROUP * DIM : (g + 1) * GROUP * DIM, :], preferred_element_type=F32)
        acc[...] = part if g == 0 else acc[...] + part

    pick_r = lax.broadcasted_iota(jnp.int32, (PAD, HROWS), 0)
    pick_c = lax.broadcasted_iota(jnp.int32, (PAD, HROWS), 1)
    low = pick_r & (BLOCK - 1)
    pick = jnp.where((low < LIVE) & (pick_r - 8 * (pick_r >> 5) == pick_c), 1.0, 0.0).astype(BF16)
    slot = lax.broadcasted_iota(jnp.int32, (8, LANES), 1)

    def evict(g):
        tally = jnp.zeros((16, TOKENS), F32)
        for i in range(GROUP):
            h = g * GROUP + i
            sides = []
            for q in range(NZ // 4):
                stats = jnp.zeros((8, LANES), F32)
                for b in range(4):
                    p = 4 * q + b
                    whole = ax[h, BLOCK * p : BLOCK * (p + 1), :].astype(F32)
                    stats = jnp.where(slot >> 5 == b, whole[LIVE:], stats)
                own = top_of(stat_v[h][:, q * LANES : (q + 1) * LANES])
                coeff = jnp.exp(own - top_of(stats)) / total_of(stats)
                sides.append(jnp.where((slot[0:1] & (BLOCK - 1)) < LIVE, coeff, 0.0))
            coeff = jnp.broadcast_to(jnp.concatenate(sides, axis=1), (16, PAD)).astype(BF16)
            coeff = jnp.dot(coeff, pick, preferred_element_type=F32).astype(BF16)
            tally = tally + jnp.dot(coeff, weights[h * HROWS : (h + 1) * HROWS, :], preferred_element_type=F32)
        if g == 0:
            ev_ref[...] = prior_ref[...] + tally[0:1]
        else:
            ev_ref[...] = ev_ref[...] + tally[0:1]

    scores(0, score_a)
    for u in range(UNITS):
        now, later = (score_a, score_b) if u % 2 == 0 else (score_b, score_a)
        if u + 1 < UNITS:
            scores(u + 1, later)
        soft(u, now)
        if u == 1:
            pl.semaphore_wait(barrier, len(peers))
        if u % 2 == 1:
            send_x(u // 2)
    for g in range(GROUPS):
        merge_x(g)
        send_z(g)
    for g in range(GROUPS):
        merge_z(g)
        share_z(g)
    for g in range(GROUPS):
        share_x(g)
    loads[3].wait()
    for g in range(GROUPS):
        gathered(g)
        project(g)
        if g + 1 < GROUPS:
            evict(g)
    hw[...] = acc[...].astype(BF16)
    for d in range(1, NHEAD):
        there = lax.rem(head + d, NHEAD)
        src = hw.at[pl.ds(pl.multiple_of(there * BLOCK, BLOCK), BLOCK)]
        sent.append(send(src, hr.at[d - 1], hs_sem.at[d - 1], hr_sem.at[d - 1], at_head(d)))
    evict(GROUPS - 1)
    final = acc[pl.ds(pl.multiple_of(head * BLOCK, BLOCK), BLOCK), :]
    for d in range(1, NHEAD):
        wait_for(hr.at[d - 1], hr_sem.at[d - 1])
        final = final + hr[d - 1].astype(F32)
    for s in range(STEPS):
        out_ref[s] = final[8 * s : 8 * s + 8].astype(BF16)
    for copy in sent:
        copy.wait_send()


def local(queries, key_latent, value_latent, key_up, value_up, out_weight, prior, lengths, positions):
    coarse, fine, freq = rotary_tables()
    vmem = pl.BlockSpec(memory_space=pltpu.VMEM)
    smem = pl.BlockSpec(memory_space=pltpu.SMEM)
    hbm = pl.BlockSpec(memory_space=pl.ANY)
    dma = pltpu.SemaphoreType.DMA
    return pl.pallas_call(
        kernel,
        out_shape=(
            jax.ShapeDtypeStruct((STEPS, ROWS // NHEAD, WIDTH), BF16),
            jax.ShapeDtypeStruct((1, TOKENS), F32),
        ),
        in_specs=[hbm, hbm, hbm, vmem, vmem, hbm, vmem, smem, vmem, vmem, vmem, vmem],
        out_specs=(vmem, vmem),
        scratch_shapes=[
            pltpu.VMEM((STEPS, ROWS, HEADS * DIM), BF16),
            pltpu.VMEM((TOKENS, RANK), BF16),
            pltpu.VMEM((TOKENS, RANK), BF16),
            pltpu.VMEM((HEADS * DIM, WIDTH), BF16),
            pltpu.VMEM((HEADS * HROWS, 2 * DIM), BF16),
            pltpu.VMEM((2 * DIM, TOKENS), BF16),
            pltpu.VMEM((TOKENS, DIM), BF16),
            pltpu.VMEM((8, LANES), F32),
            pltpu.VMEM((PAIR * HROWS, TOKENS), F32),
            pltpu.VMEM((PAIR * HROWS, TOKENS), F32),
            pltpu.VMEM((HEADS * HROWS, TOKENS), BF16),
            pltpu.VMEM((HEADS, 8, PAD), F32),
            pltpu.VMEM((HEADS, PAD, DIM), BF16),
            pltpu.VMEM((GROUPS, NX - 1, PAD, DIM), BF16),
            pltpu.VMEM((GROUPS, PAD, DIM), BF16),
            pltpu.VMEM((GROUPS, NZ - 1, BLOCK, DIM), BF16),
            pltpu.VMEM((LANES, LANES), F32),
            pltpu.VMEM((HEADS, PAD, DIM), BF16),
            pltpu.VMEM((PAD, WIDTH), F32),
            pltpu.VMEM((PAD, WIDTH), BF16),
            pltpu.VMEM((NHEAD - 1, BLOCK, WIDTH), BF16),
            dma((4,)),
            dma((GROUPS, NX - 1)),
            dma((GROUPS, NX - 1)),
            dma((GROUPS, NZ - 1)),
            dma((GROUPS, NZ - 1)),
            dma((GROUPS, NZ - 1)),
            dma((GROUPS, NZ - 1)),
            dma((GROUPS, NX - 1)),
            dma((GROUPS, NX - 1)),
            dma((NHEAD - 1,)),
            dma((NHEAD - 1,)),
        ],
        compiler_params=pltpu.CompilerParams(
            collective_id=0, has_side_effects=True, vmem_limit_bytes=56 * 2**20
        ),
        cost_estimate=pl.CostEstimate(flops=3_500_000_000, bytes_accessed=5_000_000, transcendentals=5_000_000),
        name="decode_attention",
    )(
        queries, key_latent, value_latent, key_up, value_up, out_weight, prior, lengths, positions,
        jnp.asarray(coarse), jnp.asarray(fine), jnp.asarray(freq),
    )


def solution(mesh):
    placed = (
        P(None, None, "head"),
        P("head", "ctx", None),
        P("head", "ctx", None),
        P("head", None, None),
        P("head", None, None),
        P("head", "ctx"),
        P("head", "ctx"),
        P(),
        P(),
    )
    return jax.shard_map(
        local,
        mesh=mesh,
        in_specs=placed,
        out_specs=(P(None, "head", "ctx"), P("head", "ctx")),
        check_vma=False,
    )
```

```python
import functools

import jax
import jax.numpy as jnp
import numpy as np
from jax import lax
from jax.experimental import pallas as pl
from jax.experimental.pallas import tpu as pltpu
from jax.sharding import PartitionSpec as P

ROPE_BASE = 1000000.0
NEGATIVE = -1e30
BF16 = jnp.bfloat16
F32 = jnp.float32
MESH = pl.DeviceIdType.MESH

NX, NZ, NHEAD = 4, 8, 8
STEPS, ROWS = 3, 64
HEADS, DIM, RANK = 12, 128, 256
TOKENS = 2048
WIDTH = 384
LIVE = STEPS * (ROWS // NZ)
BLOCK = LIVE + 8
PAD = NZ * BLOCK
HROWS = STEPS * ROWS
MOST = 3
GROUP = NX
GROUPS = HEADS // GROUP
UNITS = ((0, 2), (2, 2), (4, 2), (6, 2), (8, 1), (9, 1), (10, 1), (11, 1))
WIRE = HROWS + 16
FAR_X = (2, 1, 3)
AWAY = GROUPS * (NX - 1)
FAR_Z = (4, 3, 5, 2, 6, 1, 7)
FAR_HEAD = (4, 5, 3, 2, 6, 7, 1)
LANES = 128


def rotary_tables():
    half = DIM // 2
    freq = (ROPE_BASE ** (-(np.arange(half) * 2.0 / DIM))).astype(np.float32).astype(np.float64)
    starts = np.arange(NX * NZ * TOKENS // LANES, dtype=np.float64) * LANES
    coarse = freq[:, None] * starts[None, :]
    coarse = coarse.reshape(half, -1, LANES).transpose(1, 0, 2)
    fine = freq[:, None] * np.arange(LANES, dtype=np.float64)[None, :]
    pair = lambda a, axis: np.stack([np.cos(a), np.sin(a)], axis=axis).astype(np.float32)
    row = np.concatenate([freq, freq]).astype(np.float32)[None, :]
    coarse = pair(coarse, 1).reshape(-1, half, LANES)
    return np.concatenate([coarse, pair(fine, 0), np.broadcast_to(row, (1, half, DIM))], axis=0)


def three(x):
    hi = x.astype(BF16).astype(F32)
    rest = x - hi
    mid = rest.astype(BF16).astype(F32)
    return hi, mid, rest - mid


def two(x):
    hi = x.astype(BF16).astype(F32)
    return hi, x - hi


def stack_rows(rows):
    sub = lax.broadcasted_iota(jnp.int32, (8, LANES), 0)
    out = jnp.zeros((8, LANES), F32)
    for index, row in enumerate(rows):
        out = jnp.where(sub == index, row, out)
    return out


def top_of(stats):
    return stats[0:1] + stats[1:2] + stats[2:3]


def total_of(stats):
    return stats[3:4] + stats[4:5]


def join(stats):
    tops = [top_of(s) for s in stats]
    peak = functools.reduce(jnp.maximum, tops)
    factors = [jnp.exp(t - peak) for t in tops]
    total = functools.reduce(jnp.add, [f * total_of(s) for f, s in zip(factors, stats)])
    return peak, total, factors


def kernel(
    q_hbm, kl_hbm, vl_hbm, ku_hbm, vu_hbm, w_hbm, prior_hbm, len_hbm, pos_hbm, table_hbm,
    out_ref, ev_ref,
    q_v, kl_v, vl_v, ku_v, vu_v, w_v, prior_v, len_ref, pos_i, coarse, fine,
    qa, keys, values, pos_v, score_a, score_b, weights, stat_v,
    xw, xr, zw, zr, ft, ax, acc, hw, hr,
    load_sem, xs_sem, xr_sem, zs_sem, zr_sem, as_sem, ar_sem, bs_sem, br_sem,
    hs_sem, hr_sem,
):
    ctx = lax.axis_index("ctx")
    head = lax.axis_index("head")
    z = ctx // NX
    x = lax.rem(ctx, NX)

    middle = TOKENS // 2
    table = lax.div(ctx, LANES * LANES // TOKENS) * 2
    moves = [
        ("ku", ku_hbm.at[0], ku_v),
        ("kl0", kl_hbm.at[0, 0:middle], kl_v.at[0:middle]),
        ("coarse", table_hbm.at[pl.ds(table, 2)], coarse),
        ("fine", table_hbm.at[table_hbm.shape[0] - 3 :], fine),
        ("pos", pos_hbm, pos_i),
        ("len", len_hbm, len_ref),
        ("q", q_hbm, q_v),
        ("kl1", kl_hbm.at[0, middle:TOKENS], kl_v.at[middle:TOKENS]),
        ("vu", vu_hbm.at[0], vu_v),
        ("vl", vl_hbm.at[0], vl_v),
        ("w", w_hbm, w_v),
        ("prior", prior_hbm, prior_v),
    ]

    def head_at(slot):
        if slot >= AWAY:
            return (slot - AWAY) * GROUP + x
        return slot // (NX - 1) * GROUP + lax.rem(x + FAR_X[slot % (NX - 1)], NX)

    loads = {}
    for i, (name, src, dst) in enumerate(moves):
        loads[name] = pltpu.make_async_copy(src, dst, load_sem.at[i])

    def begin(*names):
        for name in names:
            loads[name].start()

    begin("ku", "kl0", "coarse", "fine", "pos", "len", "kl1", "q", "vu", "vl", "w", "prior")

    def at_x(d):
        return {"ctx": z * NX + lax.rem(x + d, NX), "head": head}

    def at_z(d):
        return {"ctx": lax.rem(z + d, NZ) * NX + x, "head": head}

    def at_head(d):
        return {"ctx": ctx, "head": lax.rem(head + d, NHEAD)}

    peers = [at_x(d) for d in range(1, NX)] + [at_z(d) for d in range(1, NZ)] + [at_head(d) for d in range(1, NHEAD)]
    barrier = pltpu.get_barrier_semaphore()
    for peer in peers:
        pl.semaphore_signal(barrier, inc=1, device_id=peer, device_id_type=MESH)

    def send(src, dst, s_sem, r_sem, peer):
        copy = pltpu.make_async_remote_copy(
            src_ref=src, dst_ref=dst, send_sem=s_sem, recv_sem=r_sem, device_id=peer, device_id_type=MESH
        )
        copy.start()
        return copy

    pos_v[...] = jnp.zeros_like(pos_v)
    loads["pos"].wait()
    loads["fine"].wait()
    pos_v[0:STEPS, 0:ROWS] = pos_i[...].astype(F32)
    pos_t = jnp.transpose(pos_v[...])
    where_at = jnp.concatenate(
        [pos_t[8 * p : 8 * p + 8, s : s + 1] for p in range(NZ) for s in range(STEPS)], axis=0
    )
    angle = where_at * fine[2, 0:1, :]
    lane = lax.broadcasted_iota(jnp.int32, (HROWS, DIM), 1)
    cos_q = jnp.cos(angle)
    sin_q = jnp.where(lane < DIM // 2, -jnp.sin(angle), jnp.sin(angle))
    row_step = jnp.concatenate(
        [jnp.full((8, DIM), s, jnp.int32) for p in range(NZ) for s in range(STEPS)], axis=0
    )
    marks = jnp.where(lane == row_step, 1.0, 0.0).astype(BF16)

    half = DIM // 2
    token = ctx * TOKENS + lax.broadcasted_iota(jnp.int32, (16, TOKENS), 1)
    step_row = lax.broadcasted_iota(jnp.int32, (16, TOKENS), 0)
    loads["len"].wait()
    limit = jnp.where(step_row == 0, len_ref[0], jnp.where(step_row == 1, len_ref[1], len_ref[2]))
    dead = (step_row < STEPS) & (token >= limit)
    keys[DIM : DIM + 16, :] = jnp.where(dead, NEGATIVE, 0.0).astype(BF16)
    keys[DIM + 16 : 2 * DIM, :] = jnp.zeros((DIM - 16, TOKENS), BF16)
    loads["ku"].wait()
    key_up = jnp.transpose(ku_v[...].astype(F32)).astype(BF16)
    loads["coarse"].wait()
    shift = lax.rem(LANES - lax.rem(ctx, LANES * LANES // TOKENS) * (TOKENS // LANES), LANES)
    cos_c = pltpu.roll(coarse[0], shift, 1)
    sin_c = pltpu.roll(coarse[1], shift, 1)
    cos_f = fine[0]
    sin_f = fine[1]
    chunk = 512
    for start in range(0, TOKENS, chunk):
        if start == 0:
            loads["kl0"].wait()
        if start == middle:
            loads["kl1"].wait()
        raw = lax.dot_general(
            key_up, kl_v[start : start + chunk, :], (((1,), (1,)), ((), ())), preferred_element_type=F32
        )
        for off in range(0, chunk, LANES):
            a = (start + off) // LANES
            ca, sa = cos_c[:, a : a + 1], sin_c[:, a : a + 1]
            cosine = ca * cos_f - sa * sin_f
            sine = sa * cos_f + ca * sin_f
            first, second = raw[:half, off : off + LANES], raw[half:, off : off + LANES]
            keys[0:half, start + off : start + off + LANES] = (first * cosine - second * sine).astype(BF16)
            keys[half:DIM, start + off : start + off + LANES] = (second * cosine + first * sine).astype(BF16)

    def turn(u):
        for h in range(UNITS[u][0], sum(UNITS[u])):
            columns = pl.ds(pl.multiple_of(head_at(h) * DIM, DIM), DIM)
            block = [q_v[s, :, columns].astype(F32) for s in range(STEPS)]
            rows = jnp.concatenate([block[s][8 * p : 8 * p + 8] for p in range(NZ) for s in range(STEPS)], axis=0)
            turned = (rows * cos_q + pltpu.roll(rows, half, 1) * sin_q) * (DIM**-0.5)
            qa[h * HROWS : (h + 1) * HROWS, 0:DIM] = turned.astype(BF16)
            qa[h * HROWS : (h + 1) * HROWS, DIM : 2 * DIM] = marks

    loads["q"].wait()
    turn(0)

    def rows_of(u):
        return slice(UNITS[u][0] * HROWS, sum(UNITS[u]) * HROWS)

    def scores(u, dst):
        dst[0 : UNITS[u][1] * HROWS, :] = jnp.dot(qa[rows_of(u), :], keys[...], preferred_element_type=F32)

    stat_lane = lax.broadcasted_iota(jnp.int32, (HROWS, LANES), 1)
    filler = jnp.where(lax.broadcasted_iota(jnp.int32, (8, LANES), 1) == 3, 1.0, 0.0)

    def soft(u, src):
        s = src[0 : UNITS[u][1] * HROWS, :]
        top = jnp.max(s, axis=1, keepdims=True)
        expo = jnp.exp(s - top)
        total = jnp.sum(expo, axis=1, keepdims=True)
        w = expo.astype(BF16)
        weights[rows_of(u), :] = w
        sums = jnp.dot(w, values[...], preferred_element_type=F32)
        for i in range(UNITS[u][1]):
            h = UNITS[u][0] + i
            rows = slice(i * HROWS, (i + 1) * HROWS)
            columns = jnp.zeros((HROWS, LANES), F32)
            for k, part in enumerate((*three(top[rows]), *two(total[rows]))):
                columns = jnp.where(stat_lane == k, part, columns)
            spread = []
            for p in range(NZ):
                spread += [columns[LIVE * p : LIVE * (p + 1)], filler]
            stats = jnp.transpose(jnp.concatenate(spread, axis=0))[0:8]
            stat_v[h] = stats
            whole = jnp.concatenate([sums[rows], stats[:, 0:LANES], stats[:, LANES:PAD]], axis=0)
            xw[h] = whole.astype(BF16)

    sent = []

    def send_x(slot):
        g, d = slot // (NX - 1), FAR_X[slot % (NX - 1)]
        sent.append(send(xw.at[slot], xr.at[g, d - 1], xs_sem.at[g, d - 1], xr_sem.at[g, d - 1], at_x(d)))

    def wait_for(dst, sem):
        pltpu.make_async_copy(dst, dst, sem).wait()

    def merge_x(g):
        for d in range(1, NX):
            wait_for(xr.at[g, d - 1], xr_sem.at[g, d - 1])
        shares = [xw[AWAY + g].astype(F32)] + [xr[g, c].astype(F32) for c in range(NX - 1)]
        by_row, stats = [], []
        for q in range(NZ // 4):
            peak, total, factors = join([s[HROWS + 8 * q : HROWS + 8 * q + 8] for s in shares])
            turned = jnp.transpose(stack_rows(factors))
            by_row += [turned[BLOCK * b : BLOCK * b + LIVE] for b in range(4)]
            stats.append(stack_rows((*three(peak), *two(total))))
        by_row = jnp.concatenate(by_row, axis=0)
        merged = functools.reduce(jnp.add, [s[:HROWS] * by_row[:, c : c + 1] for c, s in enumerate(shares)])
        blocks = []
        for p in range(NZ):
            blocks += [merged[LIVE * p : LIVE * (p + 1)], stats[p // 4]]
        zw[g] = jnp.concatenate(blocks, axis=0).astype(BF16)

    def send_z(g):
        for d in FAR_Z:
            there = lax.rem(z + d, NZ)
            src = zw.at[g, pl.ds(pl.multiple_of(there * BLOCK, BLOCK), BLOCK)]
            sent.append(send(src, zr.at[g, d - 1], zs_sem.at[g, d - 1], zr_sem.at[g, d - 1], at_z(d)))

    def mine_z():
        return pl.ds(pl.multiple_of(z * BLOCK, BLOCK), BLOCK)

    def merge_z(g):
        for d in range(1, NZ):
            wait_for(zr.at[g, d - 1], zr_sem.at[g, d - 1])
        pieces = [zw[g, mine_z(), :].astype(F32)] + [zr[g, i].astype(F32) for i in range(NZ - 1)]
        peak, total, factors = join([p[LIVE:] for p in pieces])
        scale = 1.0 / total
        ft[:, 0:8] = jnp.transpose(stack_rows([f * scale for f in factors]))
        by_row = ft[pl.ds(pl.multiple_of(lax.rem(z, 4) * BLOCK, BLOCK), LIVE), 0:8]
        merged = functools.reduce(jnp.add, [p[:LIVE] * by_row[:, c : c + 1] for c, p in enumerate(pieces)])
        stats = stack_rows((*three(peak), *two(total)))
        ax[g * GROUP + x, mine_z(), :] = jnp.concatenate([merged, stats], axis=0).astype(BF16)

    def share_z(g):
        here = ax.at[g * GROUP + x, mine_z()]
        for d in FAR_Z:
            sent.append(send(here, here, as_sem.at[g, d - 1], ar_sem.at[g, d - 1], at_z(d)))

    def share_x(g):
        for d in range(1, NZ):
            here = ax.at[g * GROUP + x, mine_z()]
            wait_for(here, ar_sem.at[g, d - 1])
        here = ax.at[g * GROUP + x]
        for d in FAR_X:
            sent.append(send(here, here, bs_sem.at[g, d - 1], br_sem.at[g, d - 1], at_x(d)))

    def gathered(g):
        for d in range(1, NX):
            here = ax.at[g * GROUP + x]
            wait_for(here, br_sem.at[g, d - 1])

    done = []

    def project(first, count):
        rows = jnp.concatenate([ax[first + i] for i in range(count)], axis=1)
        part = jnp.dot(rows, w_v[first * DIM : (first + count) * DIM, :], preferred_element_type=F32)
        acc[...] = acc[...] + part if done else part
        done.append(first)

    pick_r = lax.broadcasted_iota(jnp.int32, (PAD, HROWS), 0)
    pick_c = lax.broadcasted_iota(jnp.int32, (PAD, HROWS), 1)
    low = pick_r & (BLOCK - 1)
    pick = jnp.where((low < LIVE) & (pick_r - 8 * (pick_r >> 5) == pick_c), 1.0, 0.0).astype(BF16)
    slot = lax.broadcasted_iota(jnp.int32, (8, LANES), 1)

    tallied = []

    def evict(first, count):
        tally = jnp.zeros((16, TOKENS), F32)
        for slot_at in range(first, first + count):
            h = head_at(slot_at)
            sides = []
            for q in range(NZ // 4):
                stats = jnp.zeros((8, LANES), F32)
                for b in range(4):
                    p = 4 * q + b
                    whole = ax[h, BLOCK * p : BLOCK * (p + 1), :].astype(F32)
                    stats = jnp.where(slot >> 5 == b, whole[LIVE:], stats)
                own = top_of(stat_v[slot_at][:, q * LANES : (q + 1) * LANES])
                coeff = jnp.exp(own - top_of(stats)) / total_of(stats)
                sides.append(jnp.where((slot[0:1] & (BLOCK - 1)) < LIVE, coeff, 0.0))
            coeff = jnp.broadcast_to(jnp.concatenate(sides, axis=1), (16, PAD)).astype(BF16)
            coeff = jnp.dot(coeff, pick, preferred_element_type=F32).astype(BF16)
            tally = tally + jnp.dot(coeff, weights[slot_at * HROWS : (slot_at + 1) * HROWS, :], preferred_element_type=F32)
        ev_ref[...] = (ev_ref[...] if tallied else prior_v[...]) + tally[0:1]
        tallied.append(first)

    def drain():
        while sent:
            sent.pop(0).wait_send()

    scores(0, score_a)
    turn(1)
    loads["vu"].wait()
    loads["vl"].wait()
    values[...] = jnp.dot(vl_v[...], vu_v[...], preferred_element_type=F32).astype(BF16)
    for u in range(len(UNITS)):
        now, later = (score_a, score_b) if u % 2 == 0 else (score_b, score_a)
        if u + 2 < len(UNITS):
            turn(u + 2)
        if u + 1 < len(UNITS):
            scores(u + 1, later)
        soft(u, now)
        if u == 1:
            pl.semaphore_wait(barrier, len(peers))
        if u >= 1:
            for slot_at in range(0 if u == 1 else UNITS[u][0], min(sum(UNITS[u]), AWAY)):
                send_x(slot_at)
    for g in range(GROUPS):
        merge_x(g)
        send_z(g)
    loads["w"].wait()
    loads["prior"].wait()
    for g in range(GROUPS):
        merge_z(g)
        share_z(g)
    for g in range(GROUPS):
        share_x(g)
    drain()
    for g in range(GROUPS):
        gathered(g)
        project(g * GROUP, GROUP)
    hw[...] = acc[...].astype(BF16)
    for d in FAR_HEAD:
        there = lax.rem(head + d, NHEAD)
        src = hw.at[pl.ds(pl.multiple_of(there * BLOCK, BLOCK), BLOCK)]
        sent.append(send(src, hr.at[d - 1], hs_sem.at[d - 1], hr_sem.at[d - 1], at_head(d)))
    for g in range(GROUPS):
        evict(g * GROUP, GROUP)
    final = acc[pl.ds(pl.multiple_of(head * BLOCK, BLOCK), BLOCK), :]
    for d in range(1, NHEAD):
        wait_for(hr.at[d - 1], hr_sem.at[d - 1])
        final = final + hr[d - 1].astype(F32)
    for s in range(STEPS):
        out_ref[s] = final[8 * s : 8 * s + 8].astype(BF16)
    drain()


def finish(a_ref, b_ref, out_ref, ev_ref):
    out_ref[...] = a_ref[...]
    ev_ref[...] = b_ref[...]


def local(queries, key_latent, value_latent, key_up, value_up, out_weight, prior, lengths, positions):
    table = rotary_tables()
    vmem = pl.BlockSpec(memory_space=pltpu.VMEM)
    hbm = pl.BlockSpec(memory_space=pl.ANY)
    dma = pltpu.SemaphoreType.DMA
    shapes = (
        jax.ShapeDtypeStruct((STEPS, ROWS // NHEAD, WIDTH), BF16),
        jax.ShapeDtypeStruct((1, TOKENS), F32),
    )
    raw = pl.pallas_call(
        kernel,
        out_shape=shapes,
        in_specs=[hbm] * 10,
        out_specs=(vmem, vmem),
        scratch_shapes=[
            pltpu.VMEM((STEPS, ROWS, HEADS * DIM), BF16),
            pltpu.VMEM((TOKENS, RANK), BF16),
            pltpu.VMEM((TOKENS, RANK), BF16),
            pltpu.VMEM((RANK, DIM), BF16),
            pltpu.VMEM((RANK, DIM), BF16),
            pltpu.VMEM((HEADS * DIM, WIDTH), BF16),
            pltpu.VMEM((1, TOKENS), F32),
            pltpu.SMEM((STEPS,), jnp.int32),
            pltpu.VMEM((STEPS, ROWS), jnp.int32),
            pltpu.VMEM((2, DIM // 2, LANES), F32),
            pltpu.VMEM((3, DIM // 2, LANES), F32),
            pltpu.VMEM((HEADS * HROWS, 2 * DIM), BF16),
            pltpu.VMEM((2 * DIM, TOKENS), BF16),
            pltpu.VMEM((TOKENS, DIM), BF16),
            pltpu.VMEM((8, LANES), F32),
            pltpu.VMEM((MOST * HROWS, TOKENS), F32),
            pltpu.VMEM((MOST * HROWS, TOKENS), F32),
            pltpu.VMEM((HEADS * HROWS, TOKENS), BF16),
            pltpu.VMEM((HEADS, 8, PAD), F32),
            pltpu.VMEM((HEADS, WIRE, DIM), BF16),
            pltpu.VMEM((GROUPS, NX - 1, WIRE, DIM), BF16),
            pltpu.VMEM((GROUPS, PAD, DIM), BF16),
            pltpu.VMEM((GROUPS, NZ - 1, BLOCK, DIM), BF16),
            pltpu.VMEM((LANES, LANES), F32),
            pltpu.VMEM((HEADS, PAD, DIM), BF16),
            pltpu.VMEM((PAD, WIDTH), F32),
            pltpu.VMEM((PAD, WIDTH), BF16),
            pltpu.VMEM((NHEAD - 1, BLOCK, WIDTH), BF16),
            dma((12,)),
            dma((GROUPS, NX - 1)),
            dma((GROUPS, NX - 1)),
            dma((GROUPS, NZ - 1)),
            dma((GROUPS, NZ - 1)),
            dma((GROUPS, NZ - 1)),
            dma((GROUPS, NZ - 1)),
            dma((GROUPS, NX - 1)),
            dma((GROUPS, NX - 1)),
            dma((NHEAD - 1,)),
            dma((NHEAD - 1,)),
        ],
        compiler_params=pltpu.CompilerParams(
            collective_id=0, has_side_effects=True, vmem_limit_bytes=56 * 2**20
        ),
        cost_estimate=pl.CostEstimate(flops=3_500_000_000, bytes_accessed=5_000_000, transcendentals=5_000_000),
        name="decode_attention",
    )(
        queries, key_latent, value_latent, key_up, value_up, out_weight, prior, lengths, positions,
        jnp.asarray(table),
    )
    return pl.pallas_call(
        finish, out_shape=shapes, in_specs=[vmem, vmem], out_specs=(vmem, vmem), name="finish"
    )(*raw)


def solution(mesh):
    placed = (
        P(None, None, "head"),
        P("head", "ctx", None),
        P("head", "ctx", None),
        P("head", None, None),
        P("head", None, None),
        P("head", "ctx"),
        P("head", "ctx"),
        P(),
        P(),
    )
    return jax.shard_map(
        local,
        mesh=mesh,
        in_specs=placed,
        out_specs=(P(None, "head", "ctx"), P("head", "ctx")),
        check_vma=False,
    )
```

```python
import functools

import jax
import jax.numpy as jnp
import numpy as np
from jax import lax
from jax.experimental import pallas as pl
from jax.experimental.pallas import tpu as pltpu
from jax.sharding import PartitionSpec as P

ROPE_BASE = 1000000.0
NEGATIVE = -1e30
BF16 = jnp.bfloat16
F32 = jnp.float32
MESH = pl.DeviceIdType.MESH

NX, NZ, NHEAD = 4, 8, 8
STEPS, ROWS = 3, 64
HEADS, DIM, RANK = 12, 128, 256
TOKENS = 2048
WIDTH = 384
LIVE = STEPS * (ROWS // NZ)
BLOCK = LIVE + 8
PAD = NZ * BLOCK
HROWS = STEPS * ROWS
MOST = 3
GROUP = NX
GROUPS = HEADS // GROUP
UNITS = ((0, 2), (2, 2), (4, 2), (6, 2), (8, 1), (9, 1), (10, 1), (11, 1))
WIRE = HROWS + 16
FAR_X = (2, 1, 3)
AWAY = GROUPS * (NX - 1)
FAR_Z = (4, 3, 5, 2, 6, 1, 7)
FAR_HEAD = (4, 5, 3, 2, 6, 7, 1)
LANES = 128


def rotary_tables():
    half = DIM // 2
    freq = (ROPE_BASE ** (-(np.arange(half) * 2.0 / DIM))).astype(np.float32).astype(np.float64)
    starts = np.arange(NX * NZ * TOKENS // LANES, dtype=np.float64) * LANES
    coarse = freq[:, None] * starts[None, :]
    coarse = coarse.reshape(half, -1, LANES).transpose(1, 0, 2)
    fine = freq[:, None] * np.arange(LANES, dtype=np.float64)[None, :]
    pair = lambda a, axis: np.stack([np.cos(a), np.sin(a)], axis=axis).astype(np.float32)
    row = np.concatenate([freq, freq]).astype(np.float32)[None, :]
    coarse = pair(coarse, 1).reshape(-1, half, LANES)
    return np.concatenate([coarse, pair(fine, 0), np.broadcast_to(row, (1, half, DIM))], axis=0)


def three(x):
    hi = x.astype(BF16).astype(F32)
    rest = x - hi
    mid = rest.astype(BF16).astype(F32)
    return hi, mid, rest - mid


def two(x):
    hi = x.astype(BF16).astype(F32)
    return hi, x - hi


def stack_rows(rows):
    sub = lax.broadcasted_iota(jnp.int32, (8, LANES), 0)
    out = jnp.zeros((8, LANES), F32)
    for index, row in enumerate(rows):
        out = jnp.where(sub == index, row, out)
    return out


def top_of(stats):
    return stats[0:1] + stats[1:2] + stats[2:3]


def total_of(stats):
    return stats[3:4] + stats[4:5]


def join(stats):
    tops = [top_of(s) for s in stats]
    peak = functools.reduce(jnp.maximum, tops)
    factors = [jnp.exp(t - peak) for t in tops]
    total = functools.reduce(jnp.add, [f * total_of(s) for f, s in zip(factors, stats)])
    return peak, total, factors


def kernel(
    q_hbm, kl_hbm, vl_hbm, ku_hbm, vu_hbm, w_hbm, prior_hbm, len_hbm, pos_hbm, table_hbm,
    parts, ev_hbm,
    ev_ref, q_v, kl_v, vl_v, ku_v, vu_v, w_v, prior_v, len_ref, pos_i, coarse, fine,
    qa, keys, values, pos_v, score_a, score_b, weights, stat_v,
    xw, xr, zw, zr, ft, ax, acc, hw,
    load_sem, xs_sem, xr_sem, zs_sem, zr_sem, as_sem, ar_sem, bs_sem, br_sem,
    hs_sem, hr_sem,
):
    ctx = lax.axis_index("ctx")
    head = lax.axis_index("head")
    z = ctx // NX
    x = lax.rem(ctx, NX)

    middle = TOKENS // 2
    table = lax.div(ctx, LANES * LANES // TOKENS) * 2
    moves = [
        ("ku", ku_hbm.at[0], ku_v),
        ("kl0", kl_hbm.at[0, 0:middle], kl_v.at[0:middle]),
        ("coarse", table_hbm.at[pl.ds(table, 2)], coarse),
        ("fine", table_hbm.at[table_hbm.shape[0] - 3 :], fine),
        ("pos", pos_hbm, pos_i),
        ("len", len_hbm, len_ref),
        ("q", q_hbm, q_v),
        ("kl1", kl_hbm.at[0, middle:TOKENS], kl_v.at[middle:TOKENS]),
        ("vu", vu_hbm.at[0], vu_v),
        ("vl", vl_hbm.at[0], vl_v),
        ("w", w_hbm, w_v),
        ("prior", prior_hbm, prior_v),
    ]

    def head_at(slot):
        if slot >= AWAY:
            return (slot - AWAY) * GROUP + x
        return slot // (NX - 1) * GROUP + lax.rem(x + FAR_X[slot % (NX - 1)], NX)

    loads = {}
    for i, (name, src, dst) in enumerate(moves):
        loads[name] = pltpu.make_async_copy(src, dst, load_sem.at[i])

    def begin(*names):
        for name in names:
            loads[name].start()

    begin("ku", "kl0", "coarse", "fine", "pos", "len", "kl1", "q", "vu", "vl", "w", "prior")

    def at_x(d):
        return {"ctx": z * NX + lax.rem(x + d, NX), "head": head}

    def at_z(d):
        return {"ctx": lax.rem(z + d, NZ) * NX + x, "head": head}

    def at_head(d):
        return {"ctx": ctx, "head": lax.rem(head + d, NHEAD)}

    peers = [at_x(d) for d in range(1, NX)] + [at_z(d) for d in range(1, NZ)] + [at_head(d) for d in range(1, NHEAD)]
    barrier = pltpu.get_barrier_semaphore()
    for peer in peers:
        pl.semaphore_signal(barrier, inc=1, device_id=peer, device_id_type=MESH)

    def send(src, dst, s_sem, r_sem, peer):
        copy = pltpu.make_async_remote_copy(
            src_ref=src, dst_ref=dst, send_sem=s_sem, recv_sem=r_sem, device_id=peer, device_id_type=MESH
        )
        copy.start()
        return copy

    pos_v[...] = jnp.zeros_like(pos_v)
    loads["pos"].wait()
    loads["fine"].wait()
    pos_v[0:STEPS, 0:ROWS] = pos_i[...].astype(F32)
    pos_t = jnp.transpose(pos_v[...])
    where_at = jnp.concatenate(
        [pos_t[8 * p : 8 * p + 8, s : s + 1] for p in range(NZ) for s in range(STEPS)], axis=0
    )
    angle = where_at * fine[2, 0:1, :]
    lane = lax.broadcasted_iota(jnp.int32, (HROWS, DIM), 1)
    cos_q = jnp.cos(angle)
    sin_q = jnp.where(lane < DIM // 2, -jnp.sin(angle), jnp.sin(angle))
    row_step = jnp.concatenate(
        [jnp.full((8, DIM), s, jnp.int32) for p in range(NZ) for s in range(STEPS)], axis=0
    )
    marks = jnp.where(lane == row_step, 1.0, 0.0).astype(BF16)

    half = DIM // 2
    token = ctx * TOKENS + lax.broadcasted_iota(jnp.int32, (16, TOKENS), 1)
    step_row = lax.broadcasted_iota(jnp.int32, (16, TOKENS), 0)
    loads["len"].wait()
    limit = jnp.where(step_row == 0, len_ref[0], jnp.where(step_row == 1, len_ref[1], len_ref[2]))
    dead = (step_row < STEPS) & (token >= limit)
    keys[DIM : DIM + 16, :] = jnp.where(dead, NEGATIVE, 0.0).astype(BF16)
    keys[DIM + 16 : 2 * DIM, :] = jnp.zeros((DIM - 16, TOKENS), BF16)
    loads["ku"].wait()
    key_up = jnp.transpose(ku_v[...].astype(F32)).astype(BF16)
    loads["coarse"].wait()
    shift = lax.rem(LANES - lax.rem(ctx, LANES * LANES // TOKENS) * (TOKENS // LANES), LANES)
    cos_c = pltpu.roll(coarse[0], shift, 1)
    sin_c = pltpu.roll(coarse[1], shift, 1)
    cos_f = fine[0]
    sin_f = fine[1]
    chunk = 512
    for start in range(0, TOKENS, chunk):
        if start == 0:
            loads["kl0"].wait()
        if start == middle:
            loads["kl1"].wait()
        raw = lax.dot_general(
            key_up, kl_v[start : start + chunk, :], (((1,), (1,)), ((), ())), preferred_element_type=F32
        )
        for off in range(0, chunk, LANES):
            a = (start + off) // LANES
            ca, sa = cos_c[:, a : a + 1], sin_c[:, a : a + 1]
            cosine = ca * cos_f - sa * sin_f
            sine = sa * cos_f + ca * sin_f
            first, second = raw[:half, off : off + LANES], raw[half:, off : off + LANES]
            keys[0:half, start + off : start + off + LANES] = (first * cosine - second * sine).astype(BF16)
            keys[half:DIM, start + off : start + off + LANES] = (second * cosine + first * sine).astype(BF16)

    def turn(u):
        for h in range(UNITS[u][0], sum(UNITS[u])):
            columns = pl.ds(pl.multiple_of(head_at(h) * DIM, DIM), DIM)
            block = [q_v[s, :, columns].astype(F32) for s in range(STEPS)]
            rows = jnp.concatenate([block[s][8 * p : 8 * p + 8] for p in range(NZ) for s in range(STEPS)], axis=0)
            turned = (rows * cos_q + pltpu.roll(rows, half, 1) * sin_q) * (DIM**-0.5)
            qa[h * HROWS : (h + 1) * HROWS, 0:DIM] = turned.astype(BF16)
            qa[h * HROWS : (h + 1) * HROWS, DIM : 2 * DIM] = marks

    loads["q"].wait()
    turn(0)

    def rows_of(u):
        return slice(UNITS[u][0] * HROWS, sum(UNITS[u]) * HROWS)

    def scores(u, dst):
        dst[0 : UNITS[u][1] * HROWS, :] = jnp.dot(qa[rows_of(u), :], keys[...], preferred_element_type=F32)

    stat_lane = lax.broadcasted_iota(jnp.int32, (HROWS, LANES), 1)
    filler = jnp.where(lax.broadcasted_iota(jnp.int32, (8, LANES), 1) == 3, 1.0, 0.0)

    def soft(u, src):
        s = src[0 : UNITS[u][1] * HROWS, :]
        top = jnp.max(s, axis=1, keepdims=True)
        expo = jnp.exp(s - top)
        total = jnp.sum(expo, axis=1, keepdims=True)
        w = expo.astype(BF16)
        weights[rows_of(u), :] = w
        sums = jnp.dot(w, values[...], preferred_element_type=F32)
        for i in range(UNITS[u][1]):
            h = UNITS[u][0] + i
            rows = slice(i * HROWS, (i + 1) * HROWS)
            columns = jnp.zeros((HROWS, LANES), F32)
            for k, part in enumerate((*three(top[rows]), *two(total[rows]))):
                columns = jnp.where(stat_lane == k, part, columns)
            spread = []
            for p in range(NZ):
                spread += [columns[LIVE * p : LIVE * (p + 1)], filler]
            stats = jnp.transpose(jnp.concatenate(spread, axis=0))[0:8]
            stat_v[h] = stats
            whole = jnp.concatenate([sums[rows], stats[:, 0:LANES], stats[:, LANES:PAD]], axis=0)
            xw[h] = whole.astype(BF16)

    sent = []

    def send_x(slot):
        g, d = slot // (NX - 1), FAR_X[slot % (NX - 1)]
        sent.append(send(xw.at[slot], xr.at[g, d - 1], xs_sem.at[g, d - 1], xr_sem.at[g, d - 1], at_x(d)))

    def wait_for(dst, sem):
        pltpu.make_async_copy(dst, dst, sem).wait()

    def merge_x(g):
        for d in range(1, NX):
            wait_for(xr.at[g, d - 1], xr_sem.at[g, d - 1])
        shares = [xw[AWAY + g].astype(F32)] + [xr[g, c].astype(F32) for c in range(NX - 1)]
        by_row, stats = [], []
        for q in range(NZ // 4):
            peak, total, factors = join([s[HROWS + 8 * q : HROWS + 8 * q + 8] for s in shares])
            turned = jnp.transpose(stack_rows(factors))
            by_row += [turned[BLOCK * b : BLOCK * b + LIVE] for b in range(4)]
            stats.append(stack_rows((*three(peak), *two(total))))
        by_row = jnp.concatenate(by_row, axis=0)
        merged = functools.reduce(jnp.add, [s[:HROWS] * by_row[:, c : c + 1] for c, s in enumerate(shares)])
        blocks = []
        for p in range(NZ):
            blocks += [merged[LIVE * p : LIVE * (p + 1)], stats[p // 4]]
        zw[g] = jnp.concatenate(blocks, axis=0).astype(BF16)

    def send_z(g):
        for d in FAR_Z:
            there = lax.rem(z + d, NZ)
            src = zw.at[g, pl.ds(pl.multiple_of(there * BLOCK, BLOCK), BLOCK)]
            sent.append(send(src, zr.at[g, d - 1], zs_sem.at[g, d - 1], zr_sem.at[g, d - 1], at_z(d)))

    def mine_z():
        return pl.ds(pl.multiple_of(z * BLOCK, BLOCK), BLOCK)

    def merge_z(g):
        for d in range(1, NZ):
            wait_for(zr.at[g, d - 1], zr_sem.at[g, d - 1])
        pieces = [zw[g, mine_z(), :].astype(F32)] + [zr[g, i].astype(F32) for i in range(NZ - 1)]
        peak, total, factors = join([p[LIVE:] for p in pieces])
        scale = 1.0 / total
        ft[:, 0:8] = jnp.transpose(stack_rows([f * scale for f in factors]))
        by_row = ft[pl.ds(pl.multiple_of(lax.rem(z, 4) * BLOCK, BLOCK), LIVE), 0:8]
        merged = functools.reduce(jnp.add, [p[:LIVE] * by_row[:, c : c + 1] for c, p in enumerate(pieces)])
        stats = stack_rows((*three(peak), *two(total)))
        ax[g * GROUP + x, mine_z(), :] = jnp.concatenate([merged, stats], axis=0).astype(BF16)

    def share_z(g):
        here = ax.at[g * GROUP + x, mine_z()]
        for d in FAR_Z:
            sent.append(send(here, here, as_sem.at[g, d - 1], ar_sem.at[g, d - 1], at_z(d)))

    def share_x(g):
        for d in range(1, NZ):
            here = ax.at[g * GROUP + x, mine_z()]
            wait_for(here, ar_sem.at[g, d - 1])
        here = ax.at[g * GROUP + x]
        for d in FAR_X:
            sent.append(send(here, here, bs_sem.at[g, d - 1], br_sem.at[g, d - 1], at_x(d)))

    def gathered(g):
        for d in range(1, NX):
            here = ax.at[g * GROUP + x]
            wait_for(here, br_sem.at[g, d - 1])

    done = []

    def project(first, count):
        rows = jnp.concatenate([ax[first + i] for i in range(count)], axis=1)
        part = jnp.dot(rows, w_v[first * DIM : (first + count) * DIM, :], preferred_element_type=F32)
        acc[...] = acc[...] + part if done else part
        done.append(first)

    pick_r = lax.broadcasted_iota(jnp.int32, (PAD, HROWS), 0)
    pick_c = lax.broadcasted_iota(jnp.int32, (PAD, HROWS), 1)
    low = pick_r & (BLOCK - 1)
    pick = jnp.where((low < LIVE) & (pick_r - 8 * (pick_r >> 5) == pick_c), 1.0, 0.0).astype(BF16)
    slot = lax.broadcasted_iota(jnp.int32, (8, LANES), 1)

    tallied = []

    def evict(first, count):
        tally = jnp.zeros((16, TOKENS), F32)
        for slot_at in range(first, first + count):
            h = head_at(slot_at)
            sides = []
            for q in range(NZ // 4):
                stats = jnp.zeros((8, LANES), F32)
                for b in range(4):
                    p = 4 * q + b
                    whole = ax[h, BLOCK * p : BLOCK * (p + 1), :].astype(F32)
                    stats = jnp.where(slot >> 5 == b, whole[LIVE:], stats)
                own = top_of(stat_v[slot_at][:, q * LANES : (q + 1) * LANES])
                coeff = jnp.exp(own - top_of(stats)) / total_of(stats)
                sides.append(jnp.where((slot[0:1] & (BLOCK - 1)) < LIVE, coeff, 0.0))
            coeff = jnp.broadcast_to(jnp.concatenate(sides, axis=1), (16, PAD)).astype(BF16)
            coeff = jnp.dot(coeff, pick, preferred_element_type=F32).astype(BF16)
            tally = tally + jnp.dot(coeff, weights[slot_at * HROWS : (slot_at + 1) * HROWS, :], preferred_element_type=F32)
        ev_ref[...] = (ev_ref[...] if tallied else prior_v[...]) + tally[0:1]
        tallied.append(first)

    def drain():
        while sent:
            sent.pop(0).wait_send()

    scores(0, score_a)
    turn(1)
    loads["vu"].wait()
    loads["vl"].wait()
    values[...] = jnp.dot(vl_v[...], vu_v[...], preferred_element_type=F32).astype(BF16)
    for u in range(len(UNITS)):
        now, later = (score_a, score_b) if u % 2 == 0 else (score_b, score_a)
        if u + 2 < len(UNITS):
            turn(u + 2)
        if u + 1 < len(UNITS):
            scores(u + 1, later)
        soft(u, now)
        if u == 1:
            pl.semaphore_wait(barrier, len(peers))
        if u >= 1:
            for slot_at in range(0 if u == 1 else UNITS[u][0], min(sum(UNITS[u]), AWAY)):
                send_x(slot_at)
    for g in range(GROUPS):
        merge_x(g)
        send_z(g)
    loads["w"].wait()
    loads["prior"].wait()
    for g in range(GROUPS):
        merge_z(g)
        share_z(g)
    for g in range(GROUPS):
        share_x(g)
    drain()
    for g in range(GROUPS):
        gathered(g)
        project(g * GROUP, GROUP)
    hw[...] = acc[...].astype(BF16)

    def product(owner):
        return hw.at[pl.ds(pl.multiple_of(owner * BLOCK, BLOCK), BLOCK)]

    for d in FAR_HEAD:
        src = product(lax.rem(head + d, NHEAD))
        sent.append(send(src, parts.at[d], hs_sem.at[d - 1], hr_sem.at[d - 1], at_head(d)))
    own = pltpu.make_async_copy(product(head), parts.at[0], load_sem.at[0])
    own.start()
    for g in range(GROUPS):
        evict(g * GROUP, GROUP)
    tally = pltpu.make_async_copy(ev_ref, ev_hbm, load_sem.at[1])
    tally.start()
    drain()
    own.wait()
    tally.wait()
    for d in FAR_HEAD[::-1]:
        wait_for(parts.at[d], hr_sem.at[d - 1])


def finish(parts, tally, out_ref, ev_ref):
    ev_ref[...] = tally[...]
    final = parts[0].astype(F32)
    for d in range(1, NHEAD):
        final = final + parts[d].astype(F32)
    for s in range(STEPS):
        out_ref[s] = final[8 * s : 8 * s + 8].astype(BF16)


def local(queries, key_latent, value_latent, key_up, value_up, out_weight, prior, lengths, positions):
    table = rotary_tables()
    vmem = pl.BlockSpec(memory_space=pltpu.VMEM)
    hbm = pl.BlockSpec(memory_space=pl.ANY)
    dma = pltpu.SemaphoreType.DMA
    shapes = (
        jax.ShapeDtypeStruct((STEPS, ROWS // NHEAD, WIDTH), BF16),
        jax.ShapeDtypeStruct((1, TOKENS), F32),
    )
    raw = pl.pallas_call(
        kernel,
        out_shape=(jax.ShapeDtypeStruct((NHEAD, BLOCK, WIDTH), BF16), shapes[1]),
        in_specs=[hbm] * 10,
        out_specs=(hbm, hbm),
        scratch_shapes=[
            pltpu.VMEM((1, TOKENS), F32),
            pltpu.VMEM((STEPS, ROWS, HEADS * DIM), BF16),
            pltpu.VMEM((TOKENS, RANK), BF16),
            pltpu.VMEM((TOKENS, RANK), BF16),
            pltpu.VMEM((RANK, DIM), BF16),
            pltpu.VMEM((RANK, DIM), BF16),
            pltpu.VMEM((HEADS * DIM, WIDTH), BF16),
            pltpu.VMEM((1, TOKENS), F32),
            pltpu.SMEM((STEPS,), jnp.int32),
            pltpu.VMEM((STEPS, ROWS), jnp.int32),
            pltpu.VMEM((2, DIM // 2, LANES), F32),
            pltpu.VMEM((3, DIM // 2, LANES), F32),
            pltpu.VMEM((HEADS * HROWS, 2 * DIM), BF16),
            pltpu.VMEM((2 * DIM, TOKENS), BF16),
            pltpu.VMEM((TOKENS, DIM), BF16),
            pltpu.VMEM((8, LANES), F32),
            pltpu.VMEM((MOST * HROWS, TOKENS), F32),
            pltpu.VMEM((MOST * HROWS, TOKENS), F32),
            pltpu.VMEM((HEADS * HROWS, TOKENS), BF16),
            pltpu.VMEM((HEADS, 8, PAD), F32),
            pltpu.VMEM((HEADS, WIRE, DIM), BF16),
            pltpu.VMEM((GROUPS, NX - 1, WIRE, DIM), BF16),
            pltpu.VMEM((GROUPS, PAD, DIM), BF16),
            pltpu.VMEM((GROUPS, NZ - 1, BLOCK, DIM), BF16),
            pltpu.VMEM((LANES, LANES), F32),
            pltpu.VMEM((HEADS, PAD, DIM), BF16),
            pltpu.VMEM((PAD, WIDTH), F32),
            pltpu.VMEM((PAD, WIDTH), BF16),
            dma((12,)),
            dma((GROUPS, NX - 1)),
            dma((GROUPS, NX - 1)),
            dma((GROUPS, NZ - 1)),
            dma((GROUPS, NZ - 1)),
            dma((GROUPS, NZ - 1)),
            dma((GROUPS, NZ - 1)),
            dma((GROUPS, NX - 1)),
            dma((GROUPS, NX - 1)),
            dma((NHEAD - 1,)),
            dma((NHEAD - 1,)),
        ],
        compiler_params=pltpu.CompilerParams(
            collective_id=0, has_side_effects=True, vmem_limit_bytes=56 * 2**20
        ),
        cost_estimate=pl.CostEstimate(flops=3_500_000_000, bytes_accessed=5_000_000, transcendentals=5_000_000),
        name="decode_attention",
    )(
        queries, key_latent, value_latent, key_up, value_up, out_weight, prior, lengths, positions,
        jnp.asarray(table),
    )
    return pl.pallas_call(
        finish, out_shape=shapes, in_specs=[vmem, vmem], out_specs=(vmem, vmem), name="finish"
    )(*raw)


def solution(mesh):
    placed = (
        P(None, None, "head"),
        P("head", "ctx", None),
        P("head", "ctx", None),
        P("head", None, None),
        P("head", None, None),
        P("head", "ctx"),
        P("head", "ctx"),
        P(),
        P(),
    )
    return jax.shard_map(
        local,
        mesh=mesh,
        in_specs=placed,
        out_specs=(P(None, "head", "ctx"), P("head", "ctx")),
        check_vma=False,
    )
```

```python
import functools

import jax
import jax.numpy as jnp
import numpy as np
from jax import lax
from jax.experimental import pallas as pl
from jax.experimental.pallas import tpu as pltpu
from jax.sharding import PartitionSpec as P

ROPE_BASE = 1000000.0
NEGATIVE = -1e30
BF16 = jnp.bfloat16
F32 = jnp.float32
MESH = pl.DeviceIdType.MESH

NX, NZ, NHEAD = 4, 8, 8
STEPS, ROWS = 3, 64
HEADS, DIM, RANK = 12, 128, 256
TOKENS = 2048
WIDTH = 384
LIVE = STEPS * (ROWS // NZ)
BLOCK = LIVE + 8
PAD = NZ * BLOCK
HROWS = STEPS * ROWS
MOST = 1
GROUP = NX
GROUPS = HEADS // GROUP
UNITS = tuple((slot, 1) for slot in range(HEADS))
WIRE = HROWS + 16
FAR_X = (2, 1, 3)
AWAY = GROUPS * (NX - 1)
FAR_Z = (4, 3, 5, 2, 6, 1, 7)
FAR_HEAD = (4, 5, 3, 2, 6, 7, 1)
LANES = 128


def rotary_tables():
    half = DIM // 2
    freq = (ROPE_BASE ** (-(np.arange(half) * 2.0 / DIM))).astype(np.float32).astype(np.float64)
    starts = np.arange(NX * NZ * TOKENS // LANES, dtype=np.float64) * LANES
    coarse = freq[:, None] * starts[None, :]
    coarse = coarse.reshape(half, -1, LANES).transpose(1, 0, 2)
    fine = freq[:, None] * np.arange(LANES, dtype=np.float64)[None, :]
    pair = lambda a, axis: np.stack([np.cos(a), np.sin(a)], axis=axis).astype(np.float32)
    row = np.concatenate([freq, freq]).astype(np.float32)[None, :]
    coarse = pair(coarse, 1).reshape(-1, half, LANES)
    return np.concatenate([coarse, pair(fine, 0), np.broadcast_to(row, (1, half, DIM))], axis=0)


def three(x):
    hi = x.astype(BF16).astype(F32)
    rest = x - hi
    mid = rest.astype(BF16).astype(F32)
    return hi, mid, rest - mid


def two(x):
    hi = x.astype(BF16).astype(F32)
    return hi, x - hi


def stack_rows(rows):
    sub = lax.broadcasted_iota(jnp.int32, (8, LANES), 0)
    out = jnp.zeros((8, LANES), F32)
    for index, row in enumerate(rows):
        out = jnp.where(sub == index, row, out)
    return out


def top_of(stats):
    return stats[0:1] + stats[1:2] + stats[2:3]


def total_of(stats):
    return stats[3:4] + stats[4:5]


def join(stats):
    tops = [top_of(s) for s in stats]
    peak = functools.reduce(jnp.maximum, tops)
    factors = [jnp.exp(t - peak) for t in tops]
    total = functools.reduce(jnp.add, [f * total_of(s) for f, s in zip(factors, stats)])
    return peak, total, factors


def kernel(
    q_hbm, kl_hbm, vl_hbm, ku_hbm, vu_hbm, w_hbm, prior_hbm, len_hbm, pos_hbm, table_hbm,
    parts, ev_hbm,
    ev_ref, q_v, kl_v, vl_v, ku_v, vu_v, w_v, prior_v, len_ref, pos_i, coarse, fine,
    qa, keys, values, pos_v, score_a, score_b, weights, stat_v,
    xw, xr, zw, zr, ft, ax, acc, hw,
    load_sem, xs_sem, xr_sem, zs_sem, zr_sem, as_sem, ar_sem, bs_sem, br_sem,
    hs_sem, hr_sem,
):
    ctx = lax.axis_index("ctx")
    head = lax.axis_index("head")
    z = ctx // NX
    x = lax.rem(ctx, NX)

    middle = TOKENS // 2
    table = lax.div(ctx, LANES * LANES // TOKENS) * 2
    moves = [
        ("ku", ku_hbm.at[0], ku_v),
        ("kl0", kl_hbm.at[0, 0:middle], kl_v.at[0:middle]),
        ("coarse", table_hbm.at[pl.ds(table, 2)], coarse),
        ("fine", table_hbm.at[table_hbm.shape[0] - 3 :], fine),
        ("pos", pos_hbm, pos_i),
        ("len", len_hbm, len_ref),
        ("q", q_hbm, q_v),
        ("kl1", kl_hbm.at[0, middle:TOKENS], kl_v.at[middle:TOKENS]),
        ("vu", vu_hbm.at[0], vu_v),
        ("vl", vl_hbm.at[0], vl_v),
        ("w", w_hbm, w_v),
        ("prior", prior_hbm, prior_v),
    ]

    def head_at(slot):
        if slot >= AWAY:
            return (slot - AWAY) * GROUP + x
        return slot // (NX - 1) * GROUP + lax.rem(x + FAR_X[slot % (NX - 1)], NX)

    loads = {}
    for i, (name, src, dst) in enumerate(moves):
        loads[name] = pltpu.make_async_copy(src, dst, load_sem.at[i])

    def begin(*names):
        for name in names:
            loads[name].start()

    begin("ku", "kl0", "coarse", "fine", "pos", "len", "kl1", "q", "vu", "vl", "w", "prior")

    def at_x(d):
        return {"ctx": z * NX + lax.rem(x + d, NX), "head": head}

    def at_z(d):
        return {"ctx": lax.rem(z + d, NZ) * NX + x, "head": head}

    def at_head(d):
        return {"ctx": ctx, "head": lax.rem(head + d, NHEAD)}

    peers = [at_x(d) for d in range(1, NX)] + [at_z(d) for d in range(1, NZ)] + [at_head(d) for d in range(1, NHEAD)]
    barrier = pltpu.get_barrier_semaphore()
    for peer in peers:
        pl.semaphore_signal(barrier, inc=1, device_id=peer, device_id_type=MESH)

    def send(src, dst, s_sem, r_sem, peer):
        copy = pltpu.make_async_remote_copy(
            src_ref=src, dst_ref=dst, send_sem=s_sem, recv_sem=r_sem, device_id=peer, device_id_type=MESH
        )
        copy.start()
        return copy

    pos_v[...] = jnp.zeros_like(pos_v)
    loads["pos"].wait()
    loads["fine"].wait()
    pos_v[0:STEPS, 0:ROWS] = pos_i[...].astype(F32)
    pos_t = jnp.transpose(pos_v[...])
    where_at = jnp.concatenate(
        [pos_t[8 * p : 8 * p + 8, s : s + 1] for p in range(NZ) for s in range(STEPS)], axis=0
    )
    angle = where_at * fine[2, 0:1, :]
    lane = lax.broadcasted_iota(jnp.int32, (HROWS, DIM), 1)
    cos_q = jnp.cos(angle)
    sin_q = jnp.where(lane < DIM // 2, -jnp.sin(angle), jnp.sin(angle))
    row_step = jnp.concatenate(
        [jnp.full((8, DIM), s, jnp.int32) for p in range(NZ) for s in range(STEPS)], axis=0
    )
    marks = jnp.where(lane == row_step, 1.0, 0.0).astype(BF16)

    half = DIM // 2
    token = ctx * TOKENS + lax.broadcasted_iota(jnp.int32, (16, TOKENS), 1)
    step_row = lax.broadcasted_iota(jnp.int32, (16, TOKENS), 0)
    loads["len"].wait()
    limit = jnp.where(step_row == 0, len_ref[0], jnp.where(step_row == 1, len_ref[1], len_ref[2]))
    dead = (step_row < STEPS) & (token >= limit)
    keys[DIM : DIM + 16, :] = jnp.where(dead, NEGATIVE, 0.0).astype(BF16)
    keys[DIM + 16 : 2 * DIM, :] = jnp.zeros((DIM - 16, TOKENS), BF16)
    loads["ku"].wait()
    key_up = jnp.transpose(ku_v[...].astype(F32)).astype(BF16)
    loads["coarse"].wait()
    shift = lax.rem(LANES - lax.rem(ctx, LANES * LANES // TOKENS) * (TOKENS // LANES), LANES)
    cos_c = pltpu.roll(coarse[0], shift, 1)
    sin_c = pltpu.roll(coarse[1], shift, 1)
    cos_f = fine[0]
    sin_f = fine[1]
    chunk = 512
    for start in range(0, TOKENS, chunk):
        if start == 0:
            loads["kl0"].wait()
        if start == middle:
            loads["kl1"].wait()
        raw = lax.dot_general(
            key_up, kl_v[start : start + chunk, :], (((1,), (1,)), ((), ())), preferred_element_type=F32
        )
        for off in range(0, chunk, LANES):
            a = (start + off) // LANES
            ca, sa = cos_c[:, a : a + 1], sin_c[:, a : a + 1]
            cosine = ca * cos_f - sa * sin_f
            sine = sa * cos_f + ca * sin_f
            first, second = raw[:half, off : off + LANES], raw[half:, off : off + LANES]
            keys[0:half, start + off : start + off + LANES] = (first * cosine - second * sine).astype(BF16)
            keys[half:DIM, start + off : start + off + LANES] = (second * cosine + first * sine).astype(BF16)

    def turn(u):
        for h in range(UNITS[u][0], sum(UNITS[u])):
            columns = pl.ds(pl.multiple_of(head_at(h) * DIM, DIM), DIM)
            block = [q_v[s, :, columns].astype(F32) for s in range(STEPS)]
            rows = jnp.concatenate([block[s][8 * p : 8 * p + 8] for p in range(NZ) for s in range(STEPS)], axis=0)
            turned = (rows * cos_q + pltpu.roll(rows, half, 1) * sin_q) * (DIM**-0.5)
            qa[h * HROWS : (h + 1) * HROWS, 0:DIM] = turned.astype(BF16)
            qa[h * HROWS : (h + 1) * HROWS, DIM : 2 * DIM] = marks

    loads["q"].wait()
    turn(0)

    def rows_of(u):
        return slice(UNITS[u][0] * HROWS, sum(UNITS[u]) * HROWS)

    def scores(u, dst):
        dst[0 : UNITS[u][1] * HROWS, :] = jnp.dot(qa[rows_of(u), :], keys[...], preferred_element_type=F32)

    stat_lane = lax.broadcasted_iota(jnp.int32, (HROWS, LANES), 1)
    filler = jnp.where(lax.broadcasted_iota(jnp.int32, (8, LANES), 1) == 3, 1.0, 0.0)

    def soft(u, src):
        s = src[0 : UNITS[u][1] * HROWS, :]
        top = jnp.max(s, axis=1, keepdims=True)
        expo = jnp.exp(s - top)
        total = jnp.sum(expo, axis=1, keepdims=True)
        w = expo.astype(BF16)
        weights[rows_of(u), :] = w
        sums = jnp.dot(w, values[...], preferred_element_type=F32)
        for i in range(UNITS[u][1]):
            h = UNITS[u][0] + i
            rows = slice(i * HROWS, (i + 1) * HROWS)
            columns = jnp.zeros((HROWS, LANES), F32)
            for k, part in enumerate((*three(top[rows]), *two(total[rows]))):
                columns = jnp.where(stat_lane == k, part, columns)
            spread = []
            for p in range(NZ):
                spread += [columns[LIVE * p : LIVE * (p + 1)], filler]
            stats = jnp.transpose(jnp.concatenate(spread, axis=0))[0:8]
            stat_v[h] = stats
            whole = jnp.concatenate([sums[rows], stats[:, 0:LANES], stats[:, LANES:PAD]], axis=0)
            xw[h] = whole.astype(BF16)

    sent = []

    def send_x(slot):
        g, d = slot // (NX - 1), FAR_X[slot % (NX - 1)]
        sent.append(send(xw.at[slot], xr.at[g, d - 1], xs_sem.at[g, d - 1], xr_sem.at[g, d - 1], at_x(d)))

    def wait_for(dst, sem):
        pltpu.make_async_copy(dst, dst, sem).wait()

    def merge_x(g):
        for d in range(1, NX):
            wait_for(xr.at[g, d - 1], xr_sem.at[g, d - 1])
        shares = [xw[AWAY + g].astype(F32)] + [xr[g, c].astype(F32) for c in range(NX - 1)]
        by_row, stats = [], []
        for q in range(NZ // 4):
            peak, total, factors = join([s[HROWS + 8 * q : HROWS + 8 * q + 8] for s in shares])
            turned = jnp.transpose(stack_rows(factors))
            by_row += [turned[BLOCK * b : BLOCK * b + LIVE] for b in range(4)]
            stats.append(stack_rows((*three(peak), *two(total))))
        by_row = jnp.concatenate(by_row, axis=0)
        merged = functools.reduce(jnp.add, [s[:HROWS] * by_row[:, c : c + 1] for c, s in enumerate(shares)])
        blocks = []
        for p in range(NZ):
            blocks += [merged[LIVE * p : LIVE * (p + 1)], stats[p // 4]]
        zw[g] = jnp.concatenate(blocks, axis=0).astype(BF16)

    def send_z(g):
        for d in FAR_Z:
            there = lax.rem(z + d, NZ)
            src = zw.at[g, pl.ds(pl.multiple_of(there * BLOCK, BLOCK), BLOCK)]
            sent.append(send(src, zr.at[g, d - 1], zs_sem.at[g, d - 1], zr_sem.at[g, d - 1], at_z(d)))

    def mine_z():
        return pl.ds(pl.multiple_of(z * BLOCK, BLOCK), BLOCK)

    def merge_z(g):
        for d in range(1, NZ):
            wait_for(zr.at[g, d - 1], zr_sem.at[g, d - 1])
        pieces = [zw[g, mine_z(), :].astype(F32)] + [zr[g, i].astype(F32) for i in range(NZ - 1)]
        peak, total, factors = join([p[LIVE:] for p in pieces])
        scale = 1.0 / total
        ft[:, 0:8] = jnp.transpose(stack_rows([f * scale for f in factors]))
        by_row = ft[pl.ds(pl.multiple_of(lax.rem(z, 4) * BLOCK, BLOCK), LIVE), 0:8]
        merged = functools.reduce(jnp.add, [p[:LIVE] * by_row[:, c : c + 1] for c, p in enumerate(pieces)])
        stats = stack_rows((*three(peak), *two(total)))
        ax[g * GROUP + x, mine_z(), :] = jnp.concatenate([merged, stats], axis=0).astype(BF16)

    def share_z(g):
        here = ax.at[g * GROUP + x, mine_z()]
        for d in FAR_Z:
            sent.append(send(here, here, as_sem.at[g, d - 1], ar_sem.at[g, d - 1], at_z(d)))

    def share_x(g):
        for d in range(1, NZ):
            here = ax.at[g * GROUP + x, mine_z()]
            wait_for(here, ar_sem.at[g, d - 1])
        here = ax.at[g * GROUP + x]
        for d in FAR_X:
            sent.append(send(here, here, bs_sem.at[g, d - 1], br_sem.at[g, d - 1], at_x(d)))

    def gathered(g):
        for d in range(1, NX):
            here = ax.at[g * GROUP + x]
            wait_for(here, br_sem.at[g, d - 1])

    done = []

    def project(first, count):
        rows = jnp.concatenate([ax[first + i] for i in range(count)], axis=1)
        part = jnp.dot(rows, w_v[first * DIM : (first + count) * DIM, :], preferred_element_type=F32)
        acc[...] = acc[...] + part if done else part
        done.append(first)

    pick_r = lax.broadcasted_iota(jnp.int32, (PAD, HROWS), 0)
    pick_c = lax.broadcasted_iota(jnp.int32, (PAD, HROWS), 1)
    low = pick_r & (BLOCK - 1)
    pick = jnp.where((low < LIVE) & (pick_r - 8 * (pick_r >> 5) == pick_c), 1.0, 0.0).astype(BF16)
    slot = lax.broadcasted_iota(jnp.int32, (8, LANES), 1)

    tallied = []

    def evict(first, count):
        tally = jnp.zeros((16, TOKENS), F32)
        for slot_at in range(first, first + count):
            h = head_at(slot_at)
            sides = []
            for q in range(NZ // 4):
                stats = jnp.zeros((8, LANES), F32)
                for b in range(4):
                    p = 4 * q + b
                    whole = ax[h, BLOCK * p : BLOCK * (p + 1), :].astype(F32)
                    stats = jnp.where(slot >> 5 == b, whole[LIVE:], stats)
                own = top_of(stat_v[slot_at][:, q * LANES : (q + 1) * LANES])
                coeff = jnp.exp(own - top_of(stats)) / total_of(stats)
                sides.append(jnp.where((slot[0:1] & (BLOCK - 1)) < LIVE, coeff, 0.0))
            coeff = jnp.broadcast_to(jnp.concatenate(sides, axis=1), (16, PAD)).astype(BF16)
            coeff = jnp.dot(coeff, pick, preferred_element_type=F32).astype(BF16)
            tally = tally + jnp.dot(coeff, weights[slot_at * HROWS : (slot_at + 1) * HROWS, :], preferred_element_type=F32)
        ev_ref[...] = (ev_ref[...] if tallied else prior_v[...]) + tally[0:1]
        tallied.append(first)

    def drain():
        while sent:
            sent.pop(0).wait_send()

    scores(0, score_a)
    turn(1)
    loads["vu"].wait()
    loads["vl"].wait()
    values[...] = jnp.dot(vl_v[...], vu_v[...], preferred_element_type=F32).astype(BF16)
    for u in range(len(UNITS)):
        now, later = (score_a, score_b) if u % 2 == 0 else (score_b, score_a)
        if u + 2 < len(UNITS):
            turn(u + 2)
        if u + 1 < len(UNITS):
            scores(u + 1, later)
        soft(u, now)
        if u == 1:
            pl.semaphore_wait(barrier, len(peers))
        if u >= 1:
            for slot_at in range(0 if u == 1 else UNITS[u][0], min(sum(UNITS[u]), AWAY)):
                send_x(slot_at)
    for g in range(GROUPS):
        merge_x(g)
        send_z(g)
    loads["w"].wait()
    loads["prior"].wait()
    for g in range(GROUPS):
        merge_z(g)
        share_z(g)
    for g in range(GROUPS):
        share_x(g)
    drain()
    for g in range(GROUPS):
        gathered(g)
        project(g * GROUP, GROUP)
    hw[...] = acc[...].astype(BF16)

    def product(owner):
        return hw.at[pl.ds(pl.multiple_of(owner * BLOCK, BLOCK), BLOCK)]

    for d in FAR_HEAD:
        src = product(lax.rem(head + d, NHEAD))
        sent.append(send(src, parts.at[d], hs_sem.at[d - 1], hr_sem.at[d - 1], at_head(d)))
    own = pltpu.make_async_copy(product(head), parts.at[0], load_sem.at[0])
    own.start()
    for g in range(GROUPS):
        evict(g * GROUP, GROUP)
    tally = pltpu.make_async_copy(ev_ref, ev_hbm, load_sem.at[1])
    tally.start()
    drain()
    own.wait()
    tally.wait()
    for d in FAR_HEAD[::-1]:
        wait_for(parts.at[d], hr_sem.at[d - 1])


def finish(parts, tally, out_ref, ev_ref):
    ev_ref[...] = tally[...]
    final = parts[0].astype(F32)
    for d in range(1, NHEAD):
        final = final + parts[d].astype(F32)
    for s in range(STEPS):
        out_ref[s] = final[8 * s : 8 * s + 8].astype(BF16)


def local(queries, key_latent, value_latent, key_up, value_up, out_weight, prior, lengths, positions):
    table = rotary_tables()
    vmem = pl.BlockSpec(memory_space=pltpu.VMEM)
    hbm = pl.BlockSpec(memory_space=pl.ANY)
    dma = pltpu.SemaphoreType.DMA
    shapes = (
        jax.ShapeDtypeStruct((STEPS, ROWS // NHEAD, WIDTH), BF16),
        jax.ShapeDtypeStruct((1, TOKENS), F32),
    )
    raw = pl.pallas_call(
        kernel,
        out_shape=(jax.ShapeDtypeStruct((NHEAD, BLOCK, WIDTH), BF16), shapes[1]),
        in_specs=[hbm] * 10,
        out_specs=(hbm, hbm),
        scratch_shapes=[
            pltpu.VMEM((1, TOKENS), F32),
            pltpu.VMEM((STEPS, ROWS, HEADS * DIM), BF16),
            pltpu.VMEM((TOKENS, RANK), BF16),
            pltpu.VMEM((TOKENS, RANK), BF16),
            pltpu.VMEM((RANK, DIM), BF16),
            pltpu.VMEM((RANK, DIM), BF16),
            pltpu.VMEM((HEADS * DIM, WIDTH), BF16),
            pltpu.VMEM((1, TOKENS), F32),
            pltpu.SMEM((STEPS,), jnp.int32),
            pltpu.VMEM((STEPS, ROWS), jnp.int32),
            pltpu.VMEM((2, DIM // 2, LANES), F32),
            pltpu.VMEM((3, DIM // 2, LANES), F32),
            pltpu.VMEM((HEADS * HROWS, 2 * DIM), BF16),
            pltpu.VMEM((2 * DIM, TOKENS), BF16),
            pltpu.VMEM((TOKENS, DIM), BF16),
            pltpu.VMEM((8, LANES), F32),
            pltpu.VMEM((MOST * HROWS, TOKENS), F32),
            pltpu.VMEM((MOST * HROWS, TOKENS), F32),
            pltpu.VMEM((HEADS * HROWS, TOKENS), BF16),
            pltpu.VMEM((HEADS, 8, PAD), F32),
            pltpu.VMEM((HEADS, WIRE, DIM), BF16),
            pltpu.VMEM((GROUPS, NX - 1, WIRE, DIM), BF16),
            pltpu.VMEM((GROUPS, PAD, DIM), BF16),
            pltpu.VMEM((GROUPS, NZ - 1, BLOCK, DIM), BF16),
            pltpu.VMEM((LANES, LANES), F32),
            pltpu.VMEM((HEADS, PAD, DIM), BF16),
            pltpu.VMEM((PAD, WIDTH), F32),
            pltpu.VMEM((PAD, WIDTH), BF16),
            dma((12,)),
            dma((GROUPS, NX - 1)),
            dma((GROUPS, NX - 1)),
            dma((GROUPS, NZ - 1)),
            dma((GROUPS, NZ - 1)),
            dma((GROUPS, NZ - 1)),
            dma((GROUPS, NZ - 1)),
            dma((GROUPS, NX - 1)),
            dma((GROUPS, NX - 1)),
            dma((NHEAD - 1,)),
            dma((NHEAD - 1,)),
        ],
        compiler_params=pltpu.CompilerParams(
            collective_id=0, has_side_effects=True, vmem_limit_bytes=56 * 2**20
        ),
        cost_estimate=pl.CostEstimate(flops=3_500_000_000, bytes_accessed=5_000_000, transcendentals=5_000_000),
        name="decode_attention",
    )(
        queries, key_latent, value_latent, key_up, value_up, out_weight, prior, lengths, positions,
        jnp.asarray(table),
    )
    return pl.pallas_call(
        finish, out_shape=shapes, in_specs=[vmem, vmem], out_specs=(vmem, vmem), name="finish"
    )(*raw)


def solution(mesh):
    placed = (
        P(None, None, "head"),
        P("head", "ctx", None),
        P("head", "ctx", None),
        P("head", None, None),
        P("head", None, None),
        P("head", "ctx"),
        P("head", "ctx"),
        P(),
        P(),
    )
    return jax.shard_map(
        local,
        mesh=mesh,
        in_specs=placed,
        out_specs=(P(None, "head", "ctx"), P("head", "ctx")),
        check_vma=False,
    )
```

```python
import functools

import jax
import jax.numpy as jnp
import numpy as np
from jax import lax
from jax.experimental import pallas as pl
from jax.experimental.pallas import tpu as pltpu
from jax.sharding import PartitionSpec as P

ROPE_BASE = 1000000.0
NEGATIVE = -1e30
BF16 = jnp.bfloat16
F32 = jnp.float32
MESH = pl.DeviceIdType.MESH

NX, NZ, NHEAD = 4, 8, 8
STEPS, ROWS = 3, 64
HEADS, DIM, RANK = 12, 128, 256
TOKENS = 2048
WIDTH = 384
LIVE = STEPS * (ROWS // NZ)
BLOCK = LIVE + 8
PAD = NZ * BLOCK
HROWS = STEPS * ROWS
MOST = 1
GROUP = NX
GROUPS = HEADS // GROUP
UNITS = tuple((slot, 1) for slot in range(HEADS))
WIRE = HROWS + 16
FAR_X = (2, 1, 3)
AWAY = GROUPS * (NX - 1)
FAR_Z = (4, 3, 5, 2, 6, 1, 7)
FAR_HEAD = (4, 5, 3, 2, 6, 7, 1)
LANES = 128


def rotary_tables():
    half = DIM // 2
    freq = (ROPE_BASE ** (-(np.arange(half) * 2.0 / DIM))).astype(np.float32).astype(np.float64)
    starts = np.arange(NX * NZ * TOKENS // LANES, dtype=np.float64) * LANES
    coarse = freq[:, None] * starts[None, :]
    coarse = coarse.reshape(half, -1, LANES).transpose(1, 0, 2)
    fine = freq[:, None] * np.arange(LANES, dtype=np.float64)[None, :]
    pair = lambda a, axis: np.stack([np.cos(a), np.sin(a)], axis=axis).astype(np.float32)
    row = np.concatenate([freq, freq]).astype(np.float32)[None, :]
    coarse = pair(coarse, 1).reshape(-1, half, LANES)
    return np.concatenate([coarse, pair(fine, 0), np.broadcast_to(row, (1, half, DIM))], axis=0)


def three(x):
    hi = x.astype(BF16).astype(F32)
    rest = x - hi
    mid = rest.astype(BF16).astype(F32)
    return hi, mid, rest - mid


def two(x):
    hi = x.astype(BF16).astype(F32)
    return hi, x - hi


def stack_rows(rows):
    sub = lax.broadcasted_iota(jnp.int32, (8, LANES), 0)
    out = jnp.zeros((8, LANES), F32)
    for index, row in enumerate(rows):
        out = jnp.where(sub == index, row, out)
    return out


def top_of(stats):
    return stats[0:1] + stats[1:2] + stats[2:3]


def total_of(stats):
    return stats[3:4] + stats[4:5]


def join(stats):
    tops = [top_of(s) for s in stats]
    peak = functools.reduce(jnp.maximum, tops)
    factors = [jnp.exp(t - peak) for t in tops]
    total = functools.reduce(jnp.add, [f * total_of(s) for f, s in zip(factors, stats)])
    return peak, total, factors


def kernel(
    q_hbm, kl_hbm, vl_hbm, ku_hbm, vu_hbm, w_hbm, prior_hbm, len_hbm, pos_hbm, table_hbm,
    parts, ev_hbm,
    ev_ref, q_v, kl_v, vl_v, ku_v, vu_v, w_v, prior_v, len_ref, pos_i, coarse, fine,
    qa, keys, values, pos_v, score_a, score_b, weights, stat_v,
    xw, xr, zw, zr, ft, ax, acc, hw,
    load_sem, xs_sem, xr_sem, zs_sem, zr_sem, as_sem, ar_sem, bs_sem, br_sem,
    hs_sem, hr_sem,
):
    ctx = lax.axis_index("ctx")
    head = lax.axis_index("head")
    z = ctx // NX
    x = lax.rem(ctx, NX)

    middle = TOKENS // 2
    table = lax.div(ctx, LANES * LANES // TOKENS) * 2
    moves = [
        ("ku", ku_hbm.at[0], ku_v),
        ("kl0", kl_hbm.at[0, 0:middle], kl_v.at[0:middle]),
        ("coarse", table_hbm.at[pl.ds(table, 2)], coarse),
        ("fine", table_hbm.at[table_hbm.shape[0] - 3 :], fine),
        ("pos", pos_hbm, pos_i),
        ("len", len_hbm, len_ref),
        ("q", q_hbm, q_v),
        ("kl1", kl_hbm.at[0, middle:TOKENS], kl_v.at[middle:TOKENS]),
        ("vu", vu_hbm.at[0], vu_v),
        ("vl", vl_hbm.at[0], vl_v),
        ("w", w_hbm, w_v),
        ("prior", prior_hbm, prior_v),
    ]

    def head_at(slot):
        if slot >= AWAY:
            return (slot - AWAY) * GROUP + x
        return slot // (NX - 1) * GROUP + lax.rem(x + FAR_X[slot % (NX - 1)], NX)

    loads = {}
    for i, (name, src, dst) in enumerate(moves):
        loads[name] = pltpu.make_async_copy(src, dst, load_sem.at[i])

    def begin(*names):
        for name in names:
            loads[name].start()

    begin("ku", "kl0", "coarse", "fine", "pos", "len", "kl1", "q", "vu", "vl", "w", "prior")

    def at_x(d):
        return {"ctx": z * NX + lax.rem(x + d, NX), "head": head}

    def at_z(d):
        return {"ctx": lax.rem(z + d, NZ) * NX + x, "head": head}

    def at_head(d):
        return {"ctx": ctx, "head": lax.rem(head + d, NHEAD)}

    peers = [at_x(d) for d in range(1, NX)] + [at_z(d) for d in range(1, NZ)] + [at_head(d) for d in range(1, NHEAD)]
    barrier = pltpu.get_barrier_semaphore()
    for peer in peers:
        pl.semaphore_signal(barrier, inc=1, device_id=peer, device_id_type=MESH)

    def send(src, dst, s_sem, r_sem, peer):
        copy = pltpu.make_async_remote_copy(
            src_ref=src, dst_ref=dst, send_sem=s_sem, recv_sem=r_sem, device_id=peer, device_id_type=MESH
        )
        copy.start()
        return copy

    pos_v[...] = jnp.zeros_like(pos_v)
    loads["pos"].wait()
    loads["fine"].wait()
    pos_v[0:STEPS, 0:ROWS] = pos_i[...].astype(F32)
    pos_t = jnp.transpose(pos_v[...])
    where_at = jnp.concatenate(
        [pos_t[8 * p : 8 * p + 8, s : s + 1] for p in range(NZ) for s in range(STEPS)], axis=0
    )
    angle = where_at * fine[2, 0:1, :]
    lane = lax.broadcasted_iota(jnp.int32, (HROWS, DIM), 1)
    cos_q = jnp.cos(angle)
    sin_q = jnp.where(lane < DIM // 2, -jnp.sin(angle), jnp.sin(angle))
    row_step = jnp.concatenate(
        [jnp.full((8, DIM), s, jnp.int32) for p in range(NZ) for s in range(STEPS)], axis=0
    )
    marks = jnp.where(lane == row_step, 1.0, 0.0).astype(BF16)

    half = DIM // 2
    token = ctx * TOKENS + lax.broadcasted_iota(jnp.int32, (16, TOKENS), 1)
    step_row = lax.broadcasted_iota(jnp.int32, (16, TOKENS), 0)
    loads["len"].wait()
    limit = jnp.where(step_row == 0, len_ref[0], jnp.where(step_row == 1, len_ref[1], len_ref[2]))
    dead = (step_row < STEPS) & (token >= limit)
    keys[DIM : DIM + 16, :] = jnp.where(dead, NEGATIVE, 0.0).astype(BF16)
    keys[DIM + 16 : 2 * DIM, :] = jnp.zeros((DIM - 16, TOKENS), BF16)
    loads["ku"].wait()
    key_up = jnp.transpose(ku_v[...].astype(F32)).astype(BF16)
    loads["coarse"].wait()
    shift = lax.rem(LANES - lax.rem(ctx, LANES * LANES // TOKENS) * (TOKENS // LANES), LANES)
    cos_c = pltpu.roll(coarse[0], shift, 1)
    sin_c = pltpu.roll(coarse[1], shift, 1)
    cos_f = fine[0]
    sin_f = fine[1]
    chunk = 512
    for start in range(0, TOKENS, chunk):
        if start == 0:
            loads["kl0"].wait()
        if start == middle:
            loads["kl1"].wait()
        raw = lax.dot_general(
            key_up, kl_v[start : start + chunk, :], (((1,), (1,)), ((), ())), preferred_element_type=F32
        )
        for off in range(0, chunk, LANES):
            a = (start + off) // LANES
            ca, sa = cos_c[:, a : a + 1], sin_c[:, a : a + 1]
            cosine = ca * cos_f - sa * sin_f
            sine = sa * cos_f + ca * sin_f
            first, second = raw[:half, off : off + LANES], raw[half:, off : off + LANES]
            keys[0:half, start + off : start + off + LANES] = (first * cosine - second * sine).astype(BF16)
            keys[half:DIM, start + off : start + off + LANES] = (second * cosine + first * sine).astype(BF16)

    def turn(u):
        for h in range(UNITS[u][0], sum(UNITS[u])):
            columns = pl.ds(pl.multiple_of(head_at(h) * DIM, DIM), DIM)
            block = [q_v[s, :, columns].astype(F32) for s in range(STEPS)]
            rows = jnp.concatenate([block[s][8 * p : 8 * p + 8] for p in range(NZ) for s in range(STEPS)], axis=0)
            turned = (rows * cos_q + pltpu.roll(rows, half, 1) * sin_q) * (DIM**-0.5)
            qa[h * HROWS : (h + 1) * HROWS, 0:DIM] = turned.astype(BF16)
            qa[h * HROWS : (h + 1) * HROWS, DIM : 2 * DIM] = marks

    loads["q"].wait()
    turn(0)

    def rows_of(u):
        return slice(UNITS[u][0] * HROWS, sum(UNITS[u]) * HROWS)

    def scores(u, dst):
        dst[0 : UNITS[u][1] * HROWS, :] = jnp.dot(qa[rows_of(u), :], keys[...], preferred_element_type=F32)

    stat_lane = lax.broadcasted_iota(jnp.int32, (HROWS, LANES), 1)
    filler = jnp.where(lax.broadcasted_iota(jnp.int32, (8, LANES), 1) == 3, 1.0, 0.0)

    def soft(u, src):
        s = src[0 : UNITS[u][1] * HROWS, :]
        top = jnp.max(s, axis=1, keepdims=True)
        expo = jnp.exp(s - top)
        total = jnp.sum(expo, axis=1, keepdims=True)
        w = expo.astype(BF16)
        weights[rows_of(u), :] = w
        sums = jnp.dot(w, values[...], preferred_element_type=F32)
        for i in range(UNITS[u][1]):
            h = UNITS[u][0] + i
            rows = slice(i * HROWS, (i + 1) * HROWS)
            columns = jnp.zeros((HROWS, LANES), F32)
            for k, part in enumerate((*three(top[rows]), *two(total[rows]))):
                columns = jnp.where(stat_lane == k, part, columns)
            spread = []
            for p in range(NZ):
                spread += [columns[LIVE * p : LIVE * (p + 1)], filler]
            stats = jnp.transpose(jnp.concatenate(spread, axis=0))[0:8]
            stat_v[h] = stats
            whole = jnp.concatenate([sums[rows], stats[:, 0:LANES], stats[:, LANES:PAD]], axis=0)
            xw[h] = whole.astype(BF16)

    sent = []

    def send_x(slot):
        g, d = slot // (NX - 1), FAR_X[slot % (NX - 1)]
        sent.append(send(xw.at[slot], xr.at[g, d - 1], xs_sem.at[g, d - 1], xr_sem.at[g, d - 1], at_x(d)))

    def wait_for(dst, sem):
        pltpu.make_async_copy(dst, dst, sem).wait()

    def merge_x(g):
        for d in range(1, NX):
            wait_for(xr.at[g, d - 1], xr_sem.at[g, d - 1])
        shares = [xw[AWAY + g].astype(F32)] + [xr[g, c].astype(F32) for c in range(NX - 1)]
        by_row, stats = [], []
        for q in range(NZ // 4):
            peak, total, factors = join([s[HROWS + 8 * q : HROWS + 8 * q + 8] for s in shares])
            turned = jnp.transpose(stack_rows(factors))
            by_row += [turned[BLOCK * b : BLOCK * b + LIVE] for b in range(4)]
            stats.append(stack_rows((*three(peak), *two(total))))
        by_row = jnp.concatenate(by_row, axis=0)
        merged = functools.reduce(jnp.add, [s[:HROWS] * by_row[:, c : c + 1] for c, s in enumerate(shares)])
        blocks = []
        for p in range(NZ):
            blocks += [merged[LIVE * p : LIVE * (p + 1)], stats[p // 4]]
        zw[g] = jnp.concatenate(blocks, axis=0).astype(BF16)

    def send_z(g):
        for d in FAR_Z:
            there = lax.rem(z + d, NZ)
            src = zw.at[g, pl.ds(pl.multiple_of(there * BLOCK, BLOCK), BLOCK)]
            sent.append(send(src, zr.at[g, d - 1], zs_sem.at[g, d - 1], zr_sem.at[g, d - 1], at_z(d)))

    def mine_z():
        return pl.ds(pl.multiple_of(z * BLOCK, BLOCK), BLOCK)

    def merge_z(g):
        for d in range(1, NZ):
            wait_for(zr.at[g, d - 1], zr_sem.at[g, d - 1])
        pieces = [zw[g, mine_z(), :].astype(F32)] + [zr[g, i].astype(F32) for i in range(NZ - 1)]
        peak, total, factors = join([p[LIVE:] for p in pieces])
        scale = 1.0 / total
        ft[:, 0:8] = jnp.transpose(stack_rows([f * scale for f in factors]))
        by_row = ft[pl.ds(pl.multiple_of(lax.rem(z, 4) * BLOCK, BLOCK), LIVE), 0:8]
        merged = functools.reduce(jnp.add, [p[:LIVE] * by_row[:, c : c + 1] for c, p in enumerate(pieces)])
        stats = stack_rows((*three(peak), *two(total)))
        ax[g * GROUP + x, mine_z(), :] = jnp.concatenate([merged, stats], axis=0).astype(BF16)

    def share_z(g):
        here = ax.at[g * GROUP + x, mine_z()]
        for d in FAR_Z:
            sent.append(send(here, here, as_sem.at[g, d - 1], ar_sem.at[g, d - 1], at_z(d)))

    def share_x(g):
        for d in range(1, NZ):
            here = ax.at[g * GROUP + x, mine_z()]
            wait_for(here, ar_sem.at[g, d - 1])
        here = ax.at[g * GROUP + x]
        for d in FAR_X:
            sent.append(send(here, here, bs_sem.at[g, d - 1], br_sem.at[g, d - 1], at_x(d)))

    def gathered(g):
        for d in range(1, NX):
            here = ax.at[g * GROUP + x]
            wait_for(here, br_sem.at[g, d - 1])

    done = []

    def project(first, count):
        rows = jnp.concatenate([ax[first + i] for i in range(count)], axis=1)
        part = jnp.dot(rows, w_v[first * DIM : (first + count) * DIM, :], preferred_element_type=F32)
        acc[...] = acc[...] + part if done else part
        done.append(first)

    pick_r = lax.broadcasted_iota(jnp.int32, (PAD, HROWS), 0)
    pick_c = lax.broadcasted_iota(jnp.int32, (PAD, HROWS), 1)
    low = pick_r & (BLOCK - 1)
    pick = jnp.where((low < LIVE) & (pick_r - 8 * (pick_r >> 5) == pick_c), 1.0, 0.0).astype(BF16)
    slot = lax.broadcasted_iota(jnp.int32, (8, LANES), 1)

    tallied = []

    def evict(first, count):
        tally = jnp.zeros((16, TOKENS), F32)
        for slot_at in range(first, first + count):
            h = head_at(slot_at)
            sides = []
            for q in range(NZ // 4):
                stats = jnp.zeros((8, LANES), F32)
                for b in range(4):
                    p = 4 * q + b
                    whole = ax[h, BLOCK * p : BLOCK * (p + 1), :].astype(F32)
                    stats = jnp.where(slot >> 5 == b, whole[LIVE:], stats)
                own = top_of(stat_v[slot_at][:, q * LANES : (q + 1) * LANES])
                coeff = jnp.exp(own - top_of(stats)) / total_of(stats)
                sides.append(jnp.where((slot[0:1] & (BLOCK - 1)) < LIVE, coeff, 0.0))
            coeff = jnp.broadcast_to(jnp.concatenate(sides, axis=1), (16, PAD)).astype(BF16)
            coeff = jnp.dot(coeff, pick, preferred_element_type=F32).astype(BF16)
            tally = tally + jnp.dot(coeff, weights[slot_at * HROWS : (slot_at + 1) * HROWS, :], preferred_element_type=F32)
        ev_ref[...] = (ev_ref[...] if tallied else prior_v[...]) + tally[0:1]
        tallied.append(first)

    def drain():
        while sent:
            sent.pop(0).wait_send()

    scores(0, score_a)
    turn(1)
    loads["vu"].wait()
    loads["vl"].wait()
    values[...] = jnp.dot(vl_v[...], vu_v[...], preferred_element_type=F32).astype(BF16)
    for u in range(len(UNITS)):
        now, later = (score_a, score_b) if u % 2 == 0 else (score_b, score_a)
        if u + 2 < len(UNITS):
            turn(u + 2)
        if u + 1 < len(UNITS):
            scores(u + 1, later)
        soft(u, now)
        if u == 1:
            pl.semaphore_wait(barrier, len(peers))
        if u >= 1:
            for slot_at in range(0 if u == 1 else UNITS[u][0], min(sum(UNITS[u]), AWAY)):
                send_x(slot_at)
    for g in range(GROUPS):
        merge_x(g)
        send_z(g)
    loads["w"].wait()
    loads["prior"].wait()
    for g in range(GROUPS):
        merge_z(g)
        share_z(g)
    for g in range(GROUPS):
        share_x(g)
    for g in range(GROUPS):
        gathered(g)
        project(g * GROUP, GROUP)
    hw[...] = acc[...].astype(BF16)

    def product(owner):
        return hw.at[pl.ds(pl.multiple_of(owner * BLOCK, BLOCK), BLOCK)]

    for d in FAR_HEAD:
        src = product(lax.rem(head + d, NHEAD))
        sent.append(send(src, parts.at[d], hs_sem.at[d - 1], hr_sem.at[d - 1], at_head(d)))
    own = pltpu.make_async_copy(product(head), parts.at[0], load_sem.at[0])
    own.start()
    for g in range(GROUPS):
        evict(g * GROUP, GROUP)
    tally = pltpu.make_async_copy(ev_ref, ev_hbm, load_sem.at[1])
    tally.start()
    drain()
    own.wait()
    tally.wait()
    for d in FAR_HEAD[::-1]:
        wait_for(parts.at[d], hr_sem.at[d - 1])


def finish(parts, tally, out_ref, ev_ref):
    ev_ref[...] = tally[...]
    final = parts[0].astype(F32)
    for d in range(1, NHEAD):
        final = final + parts[d].astype(F32)
    for s in range(STEPS):
        out_ref[s] = final[8 * s : 8 * s + 8].astype(BF16)


def local(queries, key_latent, value_latent, key_up, value_up, out_weight, prior, lengths, positions):
    table = rotary_tables()
    vmem = pl.BlockSpec(memory_space=pltpu.VMEM)
    hbm = pl.BlockSpec(memory_space=pl.ANY)
    dma = pltpu.SemaphoreType.DMA
    shapes = (
        jax.ShapeDtypeStruct((STEPS, ROWS // NHEAD, WIDTH), BF16),
        jax.ShapeDtypeStruct((1, TOKENS), F32),
    )
    raw = pl.pallas_call(
        kernel,
        out_shape=(jax.ShapeDtypeStruct((NHEAD, BLOCK, WIDTH), BF16), shapes[1]),
        in_specs=[hbm] * 10,
        out_specs=(hbm, hbm),
        scratch_shapes=[
            pltpu.VMEM((1, TOKENS), F32),
            pltpu.VMEM((STEPS, ROWS, HEADS * DIM), BF16),
            pltpu.VMEM((TOKENS, RANK), BF16),
            pltpu.VMEM((TOKENS, RANK), BF16),
            pltpu.VMEM((RANK, DIM), BF16),
            pltpu.VMEM((RANK, DIM), BF16),
            pltpu.VMEM((HEADS * DIM, WIDTH), BF16),
            pltpu.VMEM((1, TOKENS), F32),
            pltpu.SMEM((STEPS,), jnp.int32),
            pltpu.VMEM((STEPS, ROWS), jnp.int32),
            pltpu.VMEM((2, DIM // 2, LANES), F32),
            pltpu.VMEM((3, DIM // 2, LANES), F32),
            pltpu.VMEM((HEADS * HROWS, 2 * DIM), BF16),
            pltpu.VMEM((2 * DIM, TOKENS), BF16),
            pltpu.VMEM((TOKENS, DIM), BF16),
            pltpu.VMEM((8, LANES), F32),
            pltpu.VMEM((MOST * HROWS, TOKENS), F32),
            pltpu.VMEM((MOST * HROWS, TOKENS), F32),
            pltpu.VMEM((HEADS * HROWS, TOKENS), BF16),
            pltpu.VMEM((HEADS, 8, PAD), F32),
            pltpu.VMEM((HEADS, WIRE, DIM), BF16),
            pltpu.VMEM((GROUPS, NX - 1, WIRE, DIM), BF16),
            pltpu.VMEM((GROUPS, PAD, DIM), BF16),
            pltpu.VMEM((GROUPS, NZ - 1, BLOCK, DIM), BF16),
            pltpu.VMEM((LANES, LANES), F32),
            pltpu.VMEM((HEADS, PAD, DIM), BF16),
            pltpu.VMEM((PAD, WIDTH), F32),
            pltpu.VMEM((PAD, WIDTH), BF16),
            dma((12,)),
            dma((GROUPS, NX - 1)),
            dma((GROUPS, NX - 1)),
            dma((GROUPS, NZ - 1)),
            dma((GROUPS, NZ - 1)),
            dma((GROUPS, NZ - 1)),
            dma((GROUPS, NZ - 1)),
            dma((GROUPS, NX - 1)),
            dma((GROUPS, NX - 1)),
            dma((NHEAD - 1,)),
            dma((NHEAD - 1,)),
        ],
        compiler_params=pltpu.CompilerParams(
            collective_id=0, has_side_effects=True, vmem_limit_bytes=56 * 2**20
        ),
        cost_estimate=pl.CostEstimate(flops=3_500_000_000, bytes_accessed=5_000_000, transcendentals=5_000_000),
        name="decode_attention",
    )(
        queries, key_latent, value_latent, key_up, value_up, out_weight, prior, lengths, positions,
        jnp.asarray(table),
    )
    return pl.pallas_call(
        finish, out_shape=shapes, in_specs=[vmem, vmem], out_specs=(vmem, vmem), name="finish"
    )(*raw)


def solution(mesh):
    placed = (
        P(None, None, "head"),
        P("head", "ctx", None),
        P("head", "ctx", None),
        P("head", None, None),
        P("head", None, None),
        P("head", "ctx"),
        P("head", "ctx"),
        P(),
        P(),
    )
    return jax.shard_map(
        local,
        mesh=mesh,
        in_specs=placed,
        out_specs=(P(None, "head", "ctx"), P("head", "ctx")),
        check_vma=False,
    )
```
